512 devices in a mesh: band: 16 (over x, y_hi, core), fft: 32 (over y_lo, z).
Axes of the slice: x: 4, y: 8 (y_hi: 2, y_lo: 4; y = y_hi * 4 + y_lo), z: 8, core: 2. Of those that a mesh axis runs over, the one named last changes fastest.
Arguments:
- orbitals: float32 [32, 128, 128, 128], P('band', 'fft'), may hold values from -6 to 6
- mask: int32 [128, 128, 128], P(None, 'fft'), may hold values from 0 to 1, as said below
Outputs:
- exchange: float32 [32, 128, 128, 128], P('band', 'fft')
The draws below stay inside these ranges and needn't reach their ends.
Inputs may be any that keep to these rules, and one draw needn't show every extreme that they name: mask is symmetric under negation of the frequency: mask[a, b, c] = mask[(-a) mod 128, (-b) mod 128, (-c) mod 128]; it is 0 wherever f(a)^2 + f(b)^2 + f(c)^2 exceeds 128^2 / 4.
All inputs are finite; a program needn't handle non-finite values.
Results may differ from the reference program's by a relative error of at most 0.00013.
Values sent between devices are 32-bit elements; how exact they have to be, the bound alone decides.
No kernel may reach another device: no remote copies, remote signals or barrier semaphores. Data moves between devices by JAX's collectives and lax.ppermute only.
A program may use at most 64 MiB of HBM per device.

```python
import jax
import jax.numpy as jnp
from jax import lax

NG = 128
BG = 2
BANDS = 32
N_BAND = 16


def draw_mask(key, part):
    key = jax.random.fold_in(key, 11)
    radius_key, cells_key = jax.random.split(key)
    index_row = jnp.arange(NG, dtype=jnp.int32)
    frequency = jnp.where(index_row < NG // 2, index_row, index_row - NG)
    squared = frequency[:, None, None] ** 2 + frequency[None, :, None] ** 2 + frequency[None, None, :] ** 2
    radius = jax.random.randint(radius_key, (), NG * NG // 6, NG * NG // 4 + 1)
    kept_cells = (jax.random.randint(cells_key, (NG, NG, NG), 0, 8) > 0).astype(jnp.int32)
    mirrored = jnp.roll(jnp.flip(kept_cells, (0, 1, 2)), 1, (0, 1, 2))
    symmetric = kept_cells * mirrored
    return ((squared <= radius).astype(jnp.int32) * symmetric).astype(jnp.int32)


def block_scale(key, extent, pieces, least, top_value):
    def one(dim, shards_of):
        draws = jax.random.uniform(jax.random.fold_in(jax.random.fold_in(key, 6), dim), (shards_of,), jnp.float32, least / len(pieces), top_value / len(pieces))
        return jnp.repeat(jnp.exp(draws), extent[dim] // shards_of).reshape((-1,) + (1,) * (len(extent) - dim - 1))

    loudness = one(*pieces[0])
    for cut in pieces[1:]:
        loudness = loudness * one(*cut)
    return loudness


def centred(key, dims, scale, most, shards=(), held_as=jnp.bfloat16):
    factor_of = block_scale(key, dims, shards, -0.22, 0.18) if shards else 1.0
    values = jax.random.normal(key, dims, jnp.float32) * scale * factor_of
    return jnp.minimum(jnp.maximum(values, -most), most).astype(held_as)


def setup_inputs(seed: int = 0) -> dict:
    splits = jax.random.split(jax.random.key(seed), 3)
    orbitals = centred(splits[0], (BANDS, NG, NG, NG), 1.0, 6.0, ((0, 16), (1, 32)), jnp.float32)
    mask = draw_mask(jax.random.fold_in(splits[2], 71), 0)
    return dict(orbitals=orbitals, mask=mask)


def signed_freq(count):
    index_row = jnp.arange(count, dtype=jnp.int32)
    return jnp.where(index_row < count // 2, index_row, index_row - count).astype(jnp.float32)


def kernel_field(mask):
    frequency = signed_freq(NG)
    squared = frequency[:, None, None] ** 2 + frequency[None, :, None] ** 2 + frequency[None, None, :] ** 2
    return mask.astype(jnp.float32) / (1.0 + squared / (NG * NG / 16.0))


def reference(orbitals, mask):
    coulomb = kernel_field(mask)
    groups = orbitals.reshape((N_BAND, BG, NG, NG, NG))
    previous = jnp.roll(groups, 1, axis=0)

    def one_group(group_pair):
        resident, earlier = group_pair
        partners = jnp.concatenate([resident, earlier], axis=0)

        def one_band(orbital):
            def one_partner(total, partner):
                density = orbital * partner
                spectrum = jnp.fft.fftn(density) * coulomb
                potential = jnp.real(jnp.fft.ifftn(spectrum)).astype(jnp.float32)
                return total + potential * partner, None

            start_total = jnp.zeros((NG, NG, NG), jnp.float32)
            total, unused = lax.scan(one_partner, start_total, partners)
            return total

        return lax.map(one_band, resident)

    result = lax.map(one_group, (groups, previous))
    return (-0.5 * result).reshape((BANDS, NG, NG, NG))
```

```python
import functools
import math

import jax
import jax.numpy as jnp
import ml_dtypes
import numpy as np
from jax import lax
from jax.experimental import pallas as pl
from jax.experimental.pallas import tpu as pltpu
from jax.sharding import PartitionSpec as P

NG = 128
HALF = NG // 2
N_FFT = 32
SLAB = NG // N_FFT
LANES = 128
VMEM_LIMIT = 56 * 1024 * 1024


def kept(ky):
    return min(HALF, math.isqrt(HALF * HALF - ky * ky) + 1)


def row_sets():
    order = sorted(range(-HALF, HALF), key=lambda k: (abs(k), -k))
    first, second, rest = order[:32], order[32:64], order[64:]
    third = rest[:32]
    fourth = rest[:31:-1]
    return [first, second, third, fourth]


ROWS = row_sets()
WIDTH = (
    max(kept(k) for k in ROWS[0]),
    max(kept(k) for k in ROWS[1]),
    max(kept(a) + kept(b) for a, b in zip(ROWS[2], ROWS[3])),
)


class Plan:
    def __init__(self, count):
        lanes = []
        for field in range(count):
            for position in range(WIDTH[2]):
                lanes.append((field, 2, position))
        tight = -(-count * sum(WIDTH) // LANES) < sum(
            -(-count * width // LANES) for width in WIDTH
        )
        for kind in (1, 0):
            if not tight:
                lanes += [None] * (-len(lanes) % LANES)
            for field in range(count):
                for position in range(WIDTH[kind]):
                    lanes.append((field, kind, position))
        lanes += [None] * (-len(lanes) % LANES)
        self.count = count
        self.size = len(lanes)
        self.tiles = self.size // LANES
        self.lanes = lanes
        self.entries = []
        for tile in range(self.tiles):
            part = lanes[tile * LANES : (tile + 1) * LANES]
            for rows in range(4):
                kz_of = {}
                for lane, item in enumerate(part):
                    if item is None:
                        continue
                    field, kind, position = item
                    if kind == rows:
                        kz_of[lane] = (field, position)
                    elif kind == 2 and rows == 3:
                        kz = WIDTH[2] - 1 - position
                        if kz < kept(ROWS[3][0]) or kz < max(kept(k) for k in ROWS[3]):
                            kz_of[lane] = (field, kz)
                kz_of = {
                    lane: (field, kz)
                    for lane, (field, kz) in kz_of.items()
                    if kz < max(kept(k) for k in ROWS[rows])
                }
                if kz_of:
                    self.entries.append((tile, rows, kz_of))
        self.zero_lane = {
            item[0]: lane
            for lane, item in enumerate(lanes)
            if item is not None and item[1] == 0 and item[2] == 0
        }
        self.choice = self.pick()

    def pick(self):
        table = np.zeros((N_FFT, 4, self.size), np.float32)
        for tile, rows, kz_of in self.entries:
            for lane, (_, kz) in kz_of.items():
                for device in range(N_FFT):
                    if kz < kept(ROWS[rows][device]):
                        table[device, rows, tile * LANES + lane] = 1.0
        assert table.sum(1).max() == 1.0
        return table

    def kz_row(self, rows):
        out = np.full((self.size,), -1, np.int64)
        for tile, which, kz_of in self.entries:
            if which == rows:
                for lane, (_, kz) in kz_of.items():
                    out[tile * LANES + lane] = kz
        return out


def turn(a, b):
    angle = (np.asarray(a)[:, None] * np.asarray(b)[None, :]) % NG * (2.0 * np.pi / NG)
    return np.cos(angle), np.sin(angle)


def pair(table):
    high = table.astype(np.float32).astype(ml_dtypes.bfloat16)
    low = (table - high.astype(np.float64)).astype(np.float32).astype(ml_dtypes.bfloat16)
    return high, low


def stacked(tables):
    whole = np.concatenate(tables, axis=0)
    return np.stack(pair(whole))


@functools.lru_cache(None)
def plan_of(count):
    return Plan(count)


GRID_POINTS = np.arange(NG)


@functools.lru_cache(None)
def z_tables(count, back):
    plan = plan_of(count)
    blocks = []
    places = []
    start = 0
    for tile, rows, kz_of in plan.entries:
        fields = sorted({field for field, _ in kz_of.values()})
        table = np.zeros((len(fields), NG, 2 * LANES))
        for lane, (field, kz) in kz_of.items():
            angle = GRID_POINTS * kz % NG * (2.0 * np.pi / NG)
            spot = fields.index(field)
            cosine, sine = np.cos(angle), np.sin(angle)
            if back:
                weight = 1.0 if kz == 0 else 2.0
                table[spot, :, lane] = weight * cosine
                table[spot, :, LANES + lane] = (1.0 - 2.0 * (GRID_POINTS % 2)) if kz == 0 else -weight * sine
            else:
                table[spot, :, lane] = cosine
                table[spot, :, LANES + lane] = -sine
        if back:
            block = np.concatenate([table[i].T for i in range(len(fields))], axis=1)
            if block.shape[1] < 3 * NG:
                block = np.pad(block, ((0, 0), (0, 3 * NG - block.shape[1])))
            size = 2 * LANES
        else:
            block = table.reshape(len(fields) * NG, 2 * LANES)
            size = len(fields) * NG
        blocks.append(block)
        places.append((tile, rows, tuple(fields), start))
        start += size
    return stacked(blocks), tuple(places)


@functools.lru_cache(None)
def y_tables(back):
    blocks = []
    for rows in range(4):
        cosine, sine = turn(ROWS[rows], GRID_POINTS)
        cosine, sine = np.repeat(cosine[:, None], SLAB, 1), np.repeat(sine[:, None], SLAB, 1)
        if back:
            real = np.concatenate([cosine, -sine], 1).reshape(2 * NG, NG).T
            imag = np.concatenate([sine, cosine], 1).reshape(2 * NG, NG).T
            blocks.append(np.concatenate([real, imag], 0))
        else:
            real = np.concatenate([cosine, sine], 2)
            imag = np.concatenate([-sine, cosine], 2)
            blocks.append(np.concatenate([real, imag], 1).reshape(2 * NG, 2 * NG))
    return stacked(blocks)


@functools.lru_cache(None)
def x_tables():
    cosine, sine = turn(GRID_POINTS, GRID_POINTS)
    shape = (NG, N_FFT, SLAB)
    cosine, sine = cosine.reshape(shape), sine.reshape(shape)
    real = np.stack([cosine, sine], 2).reshape(NG, 2 * NG)
    imag = np.stack([-sine, cosine], 2).reshape(NG, 2 * NG)
    ahead = np.concatenate([real, imag], 0)
    real = np.stack([cosine, -sine], 2).reshape(NG, 2 * NG).T
    imag = np.stack([sine, cosine], 2).reshape(NG, 2 * NG).T
    back = np.concatenate([real, imag], 1)
    real_rows = np.stack([cosine, sine], 2).reshape(NG, 2 * NG).T
    del real, imag
    back = np.zeros((N_FFT, 2, SLAB, 2, NG))
    back[:, 0, :, 0] = cosine.transpose(1, 2, 0)
    back[:, 0, :, 1] = -sine.transpose(1, 2, 0)
    back[:, 1, :, 0] = sine.transpose(1, 2, 0)
    back[:, 1, :, 1] = cosine.transpose(1, 2, 0)
    del real_rows
    return stacked([ahead, back.reshape(2 * NG, 2 * NG)])


@functools.lru_cache(None)
def line_tables(count):
    plan = plan_of(count)
    out = np.zeros((N_FFT, 8, plan.size), np.float32)
    out[:, :4] = plan.choice
    for rows in range(4):
        kz = plan.kz_row(rows)
        ky = np.asarray(ROWS[rows])
        out[:, 4] += plan.choice[:, rows] * (ky[:, None] ** 2 + kz[None, :] ** 2)
    for lane in plan.zero_lane.values():
        out[0, 5, lane] = 1.0
    spread = np.zeros((2, NG, plan.size), np.float32)
    for slot, rows in ((0, (0, 1, 2)), (1, (3,))):
        for which in rows:
            for lane, kz in enumerate(plan.kz_row(which)):
                if kz >= 0:
                    spread[slot, kz, lane] = 1.0
    return out, spread.astype(ml_dtypes.bfloat16)


@functools.lru_cache(None)
def mask_rounds():
    edges = {source: [] for source in range(N_FFT)}
    for device in range(N_FFT):
        for rows in range(4):
            index = ROWS[rows][device] % NG
            edges[index // SLAB].append((device, index % SLAB, rows))
    rounds = []
    for _ in range(SLAB):
        taken = {}

        def place(source, seen):
            for edge in edges[source]:
                if edge[0] in seen:
                    continue
                seen.add(edge[0])
                if edge[0] not in taken or place(taken[edge[0]][0], seen):
                    taken[edge[0]] = (source, edge)
                    return True
            return False

        for source in range(N_FFT):
            assert place(source, set())
        pairs, local, slot = [], [0] * N_FFT, [0] * N_FFT
        for device, (source, edge) in taken.items():
            edges[source].remove(edge)
            pairs.append((source, device))
            local[source] = edge[1]
            slot[device] = edge[2]
        rounds.append((tuple(sorted(pairs)), tuple(local), tuple(slot)))
    return tuple(rounds)


def split(value):
    high = value.astype(jnp.bfloat16)
    return high, (value - high.astype(jnp.float32)).astype(jnp.bfloat16)


def dot(left, right):
    return jnp.dot(left, right, preferred_element_type=jnp.float32)


def dot3(left, right):
    return dot(left[0], right[0]) + (dot(left[1], right[0]) + dot(left[0], right[1]))


def dense(count, products):
    return [split(left * right) for left, right in products]


def ahead_kernel(places, zero_lanes, products_of, *refs):
    *inputs, z_ref, y_ref, out_ref = refs
    densities = products_of(inputs)
    halves = [split(density) for density in densities]
    row = lax.broadcasted_iota(jnp.int32, (2 * NG, LANES), 0) % SLAB
    tiles = {}
    for index, (tile, rows, fields, start) in enumerate(places):
        table = [z_ref[part, start : start + len(fields) * NG, :] for part in range(2)]
        left = [
            jnp.concatenate([halves[field][part] for field in fields], axis=1) for part in range(2)
        ]
        lines = dot3(left, table)
        real, imag = lines[:, :LANES], lines[:, LANES:]
        planes = [
            jnp.concatenate([real[NG * x : NG * x + NG], imag[NG * x : NG * x + NG]], axis=0)
            for x in range(SLAB)
        ]
        table = [y_ref[part, 2 * NG * rows : 2 * NG * (rows + 1), :] for part in range(2)]
        total = None
        for x in range(0, SLAB, 2):
            both = dot3(table, split(jnp.concatenate([planes[x], planes[x + 1]], axis=1)))
            for step in range(2):
                piece = both[:, LANES * step : LANES * (step + 1)]
                total = piece if total is None else jnp.where(row == x + step, piece, total)
        tiles.setdefault(tile, []).append((index, rows, total))
    return densities, tiles


def forward_body(plan_count, products_of, n_in, *refs):
    plan = plan_of(plan_count)
    _, places = z_tables(plan_count, False)
    pick_ref = refs[n_in + 2]
    out_ref = refs[n_in + 3]
    densities, tiles = ahead_kernel(places, None, products_of, *refs[: n_in + 2], out_ref)
    for tile, parts in tiles.items():
        lanes = slice(tile * LANES, (tile + 1) * LANES)
        value = None
        for _, rows, total in parts:
            if rows >= 2:
                total = total * pick_ref[rows - 2, :, lanes].astype(jnp.float32)
            value = total if value is None else value + total
        out_ref[:, lanes] = value
    row = lax.broadcasted_iota(jnp.int32, (2 * SLAB, LANES), 0)
    lane_of = lax.broadcasted_iota(jnp.int32, (2 * SLAB, LANES), 1)
    sign = (1 - 2 * (lax.broadcasted_iota(jnp.int32, (1, NG), 1) % 2)).astype(jnp.float32)
    for field, lane in plan.zero_lane.items():
        tile = lane // LANES
        lanes = slice(tile * LANES, (tile + 1) * LANES)
        extra = jnp.zeros((2 * SLAB, LANES), jnp.float32)
        for x in range(SLAB):
            sums = jnp.sum(densities[field][NG * x : NG * x + NG, :], axis=0, keepdims=True)
            value = jnp.sum(sums * sign, axis=1, keepdims=True)
            extra = jnp.where((row == SLAB + x) & (lane_of == lane % LANES), value, extra)
        out_ref[0 : 2 * SLAB, lanes] += extra


def middle_body(plan_count, place_ref, x_ref, mask_ref, line_ref, spread_ref, table_ref, out_ref):
    size = plan_of(plan_count).size
    masks = [mask_ref[place_ref[1 + rows]].astype(jnp.float32).astype(jnp.bfloat16) for rows in range(4)]
    zero_mask = masks[0][0:1, HALF : HALF + 1].astype(jnp.float32)
    row = lax.broadcasted_iota(jnp.int32, (2 * NG, LANES), 0)
    is_imag = (row % (2 * SLAB)) >= SLAB
    kx = lax.broadcasted_iota(jnp.int32, (NG, LANES), 0)
    signed = jnp.where(kx < HALF, kx, kx - NG).astype(jnp.float32)
    forward = [table_ref[part, : 2 * NG, :] for part in range(2)]
    inverse = [table_ref[part, 2 * NG :, :] for part in range(2)]
    step = 0
    while step < size:
        width = min(2 * LANES, size - step)
        values, weights_real, weights_imag = [], [], []
        for start in range(step, step + width, LANES):
            lanes = slice(start, start + LANES)
            value = x_ref[:, lanes]
            zero = line_ref[0, 5:6, lanes]
            mean = jnp.sum(jnp.where(is_imag, value, 0.0), axis=0, keepdims=True) * (1.0 / NG)
            values.append(jnp.where(is_imag & (zero > 0.0), mean, value))
            kept_cells = jnp.zeros((NG, LANES), jnp.float32)
            for rows in range(4):
                spread = spread_ref[1 if rows == 3 else 0, :, lanes]
                kept_cells += dot(masks[rows], spread) * line_ref[0, rows : rows + 1, lanes]
            squared = signed * signed + line_ref[0, 4:5, lanes]
            scale = (1.0 + squared / (NG * NG / 16.0)) * float(NG**3)
            weight = kept_cells / scale
            weights_real.append(weight)
            special = zero_mask / ((1.0 + HALF * HALF / (NG * NG / 16.0)) * float(NG**3))
            weights_imag.append(jnp.where((kx == 0) & (zero > 0.0), special, weight))
        join = lambda parts: parts[0] if len(parts) == 1 else jnp.concatenate(parts, axis=1)
        spectrum = dot3(forward, split(join(values)))
        weight = jnp.concatenate([join(weights_real), join(weights_imag)], axis=0)
        out_ref[:, step : step + width] = dot3(inverse, split(spectrum * weight))
        step += width


def potentials(plan_count, y_in_ref, z_ref, y_ref, pick_ref):
    _, places = z_tables(plan_count, True)
    row = lax.broadcasted_iota(jnp.int32, (2 * NG, LANES), 0) % SLAB
    result = [None] * plan_count
    for tile, rows, fields, start in places:
        lanes = slice(tile * LANES, (tile + 1) * LANES)
        value = y_in_ref[:, lanes]
        if rows >= 2:
            value = value * pick_ref[rows - 2, :, lanes].astype(jnp.float32)
        table = [y_ref[part, 2 * NG * rows : 2 * NG * (rows + 1), :] for part in range(2)]
        planes = []
        for x in range(0, SLAB, 2):
            both = jnp.concatenate(
                [jnp.where(row == x + step, value, 0.0) for step in range(2)], axis=1
            )
            both = dot3(table, split(both))
            for step in range(2):
                piece = both[:, LANES * step : LANES * (step + 1)]
                planes.append(jnp.concatenate([piece[:NG], piece[NG:]], axis=1))
        lines = split(jnp.concatenate(planes, axis=0))
        width = len(fields) * NG
        table = [z_ref[part, start : start + 2 * LANES, :width] for part in range(2)]
        grid = dot3(lines, table)
        for spot, field in enumerate(fields):
            piece = grid[:, NG * spot : NG * (spot + 1)]
            result[field] = piece if result[field] is None else result[field] + piece
    return result


def back_resident_body(own_ref, y_in_ref, z_ref, y_ref, pick_ref, out_ref):
    first, cross, second = potentials(3, y_in_ref, z_ref, y_ref, pick_ref)
    out_ref[0] = first * own_ref[0] + cross * own_ref[1]
    out_ref[1] = cross * own_ref[0] + second * own_ref[1]


def back_cross_body(other_ref, sum_ref, y_in_ref, z_ref, y_ref, pick_ref, out_ref):
    grids = potentials(4, y_in_ref, z_ref, y_ref, pick_ref)
    for band in range(2):
        total = grids[2 * band] * other_ref[0] + grids[2 * band + 1] * other_ref[1]
        out_ref[band] = -0.5 * (sum_ref[band] + total)


def resident_products(refs):
    (own,) = refs
    return [own[0] * own[0], own[0] * own[1], own[1] * own[1]]


def cross_products(refs):
    own, other = refs
    return [own[b] * other[j] for b in range(2) for j in range(2)]


def pick_table(count):
    choice = plan_of(count).choice[:, 2:4]
    rows = np.repeat(choice.transpose(1, 0, 2), 2 * SLAB, axis=1)
    return rows.astype(ml_dtypes.bfloat16)


def call(body, shape, args, flops, name):
    moved = sum(arg.size * arg.dtype.itemsize for arg in args) + 4 * math.prod(shape)
    return pl.pallas_call(
        body,
        out_shape=jax.ShapeDtypeStruct(shape, jnp.float32),
        in_specs=[pl.BlockSpec(memory_space=pltpu.VMEM) for _ in args],
        out_specs=pl.BlockSpec(memory_space=pltpu.VMEM),
        compiler_params=pltpu.CompilerParams(vmem_limit_bytes=VMEM_LIMIT),
        cost_estimate=pl.CostEstimate(flops=flops, bytes_accessed=moved, transcendentals=0),
        name=name,
    )(*args)


def ahead(count, products_of, grids, name):
    plan = plan_of(count)
    table, _ = z_tables(count, False)
    args = [*grids, jnp.asarray(table), jnp.asarray(y_tables(False)), jnp.asarray(pick_table(count))]
    body = functools.partial(forward_body, count, products_of, len(grids))
    return call(body, (2 * NG, plan.size), args, 3 * 10**8 * len(plan.entries), name)


def middle(count, values, masks, places, name):
    plan = plan_of(count)
    lines, spread = line_tables(count)
    whole = lambda *shape: pl.BlockSpec(shape, lambda i, place: (0,) * len(shape))
    table = x_tables()
    return pl.pallas_call(
        functools.partial(middle_body, count),
        out_shape=jax.ShapeDtypeStruct((2 * NG, plan.size), jnp.float32),
        grid_spec=pltpu.PrefetchScalarGridSpec(
            num_scalar_prefetch=1,
            grid=(1,),
            in_specs=[
                whole(2 * NG, plan.size),
                whole(4, NG, NG),
                pl.BlockSpec((1, 8, plan.size), lambda i, place: (place[0], 0, 0)),
                whole(2, NG, plan.size),
                whole(2, 4 * NG, 2 * NG),
            ],
            out_specs=whole(2 * NG, plan.size),
        ),
        compiler_params=pltpu.CompilerParams(vmem_limit_bytes=VMEM_LIMIT),
        cost_estimate=pl.CostEstimate(
            flops=3 * 4 * 65536 * plan.size, bytes_accessed=8 * 256 * plan.size, transcendentals=0
        ),
        name=name,
    )(places, values, masks, jnp.asarray(lines), jnp.asarray(spread), jnp.asarray(table))


def back(body, count, grids, values, name):
    plan = plan_of(count)
    table, _ = z_tables(count, True)
    args = [*grids, values, jnp.asarray(table), jnp.asarray(y_tables(True)), jnp.asarray(pick_table(count))]
    return call(body, (2, SLAB * NG, NG), args, 3 * 10**8 * len(plan.entries), name)


def swap(values):
    size = values.shape[1]
    blocks = values.reshape(N_FFT, 2 * SLAB, size)
    blocks = lax.all_to_all(blocks, "fft", split_axis=0, concat_axis=0, tiled=True)
    return blocks.reshape(2 * NG, size)


def mask_rows(mask, me):
    arrived = []
    slots = []
    for pairs, local, slot in mask_rounds():
        start = jnp.asarray(local, jnp.int32)[me]
        sent = lax.dynamic_index_in_dim(mask, start, axis=1, keepdims=False)
        arrived.append(lax.ppermute(sent, "fft", pairs))
        slots.append(slot)
    order = np.argsort(np.asarray(slots).T, axis=1).astype(np.int32)
    return jnp.stack(arrived), order


def body(orbitals, mask):
    me = lax.axis_index("fft")
    count = lax.axis_size("band")
    other = lax.ppermute(orbitals, "band", [(i, (i + 1) % count) for i in range(count)])
    own = orbitals.reshape(2, SLAB * NG, NG)
    other = other.reshape(2, SLAB * NG, NG)

    sent_own = ahead(3, resident_products, (own,), "ahead_own")
    sent_own, mask = lax.optimization_barrier((sent_own, mask))
    lines_own = swap(sent_own)
    masks, order = mask_rows(mask, me)
    places = jnp.concatenate([me[None].astype(jnp.int32), jnp.asarray(order)[me]])
    lines_cross = swap(ahead(4, cross_products, (own, other), "ahead_cross"))
    lines_own = swap(middle(3, lines_own, masks, places, "middle_own"))
    lines_cross = swap(middle(4, lines_cross, masks, places, "middle_cross"))
    total = back(back_resident_body, 3, (own,), lines_own, "back_own")
    total = back(back_cross_body, 4, (other, total), lines_cross, "back_cross")
    return total.reshape(orbitals.shape)


def solution(mesh):
    in_specs = (P("band", "fft", None, None), P(None, "fft", None))
    out_specs = P("band", "fft", None, None)
    return jax.shard_map(body, mesh=mesh, in_specs=in_specs, out_specs=out_specs, check_vma=False)
```

```python
import functools
import math

import jax
import jax.numpy as jnp
import ml_dtypes
import numpy as np
from jax import lax
from jax.experimental import pallas as pl
from jax.experimental.pallas import tpu as pltpu
from jax.sharding import PartitionSpec as P

NG = 128
HALF = NG // 2
N_FFT = 32
SLAB = NG // N_FFT
BLOCK = 2 * SLAB
LANES = 128
ROWS_ALL = 4 * 2 * NG
NO_LINE = 999
VMEM_LIMIT = 20 * 1024 * 1024


def kept(ky):
    return min(HALF, math.isqrt(HALF * HALF - ky * ky) + 1)


def row_sets():
    order = sorted(range(-HALF, HALF), key=lambda k: (abs(k), -k))
    return [order[:32], order[32:64], order[64:96], order[:95:-1]]


KY = row_sets()
WIDE = [max(kept(k) for k in KY[0]), max(kept(k) for k in KY[1])]
SHARED = max(kept(a) + kept(b) for a, b in zip(KY[2], KY[3]))


def layout(count):
    if count == 3:
        rest = NG // 2 - WIDE[1]
        tail = 3 * SHARED - 2 * LANES
        assert 0 <= tail <= rest
        pieces = [(0, f, 0, WIDE[0], HALF * f) for f in range(3)]
        pieces += [(1, 2, 0, WIDE[1], 3 * HALF), (2, 2, SHARED - tail, tail, 3 * HALF + WIDE[1])]
        pieces += [(1, f, 0, WIDE[1], 4 * HALF + HALF * f) for f in range(2)]
        start = 6 * HALF
        pieces += [(2, f, 0, SHARED - (tail if f == 2 else 0), start + SHARED * f) for f in range(3)]
        size = start + 2 * LANES
    else:
        pieces = [(0, f, 0, WIDE[0], HALF * f) for f in range(4)]
        pieces += [(1, f, 0, WIDE[1], HALF * (4 + f)) for f in range(4)]
        pieces += [(2, f, 0, SHARED, 8 * HALF + 96 * f) for f in range(4)]
        size = 7 * LANES
    cut = []
    for kind, field, first, lanes, place in pieces:
        while lanes:
            step = min(lanes, LANES - place % LANES)
            cut.append((kind, field, first, step, place))
            first, lanes, place = first + step, lanes - step, place + step
    return cut, size


@functools.lru_cache(None)
def lane_rows(count):
    pieces, size = layout(count)
    out = np.full((8, size), NO_LINE, np.int32)
    for kind, _, first, lanes, place in pieces:
        spots = np.arange(lanes)
        out[kind, place + spots] = first + spots
        if kind == 2:
            out[3, place + spots] = SHARED - 1 - first - spots
    return out


def turn(a, b):
    angle = (np.asarray(a)[:, None] * np.asarray(b)[None, :]) % NG * (2.0 * np.pi / NG)
    return np.cos(angle), np.sin(angle)


def pair(table):
    high = table.astype(np.float32).astype(ml_dtypes.bfloat16)
    low = (table - high.astype(np.float64)).astype(np.float32).astype(ml_dtypes.bfloat16)
    return np.stack([high, low])


POINTS = np.arange(NG)


@functools.lru_cache(None)
def y_table():
    cosine, sine = turn(np.concatenate(KY), POINTS)
    return np.stack([cosine, -sine], 1).reshape(2 * NG, NG)


def doubled(block):
    return np.kron(np.eye(2), block)


@functools.lru_cache(None)
def z_ahead():
    out = []
    for kz in (np.arange(HALF), np.arange(HALF)[::-1]):
        cosine, sine = turn(POINTS, kz)
        out.append(np.concatenate([doubled(cosine), doubled(sine)], 1))
    return np.concatenate(out, 0)


@functools.lru_cache(None)
def z_back():
    out = []
    for kz in (np.arange(HALF), np.arange(HALF)[::-1]):
        cosine, sine = turn(kz, POINTS)
        weight = np.where(kz == 0, 1.0, 2.0)[:, None]
        cosine, sine = weight * cosine, weight * sine
        sine[kz == 0] = -(1.0 - 2.0 * (POINTS % 2))
        out.append(np.concatenate([doubled(cosine), doubled(sine)], 0))
    return np.concatenate(out, 0)


@functools.lru_cache(None)
def x_tables():
    cosine, sine = turn(POINTS, POINTS)
    ahead = np.zeros((2, NG, N_FFT, 2, SLAB))
    split_planes = lambda table: table.reshape(NG, N_FFT, SLAB)
    ahead[0, :, :, 0] = split_planes(cosine)
    ahead[0, :, :, 1] = split_planes(sine)
    ahead[1, :, :, 0] = split_planes(-sine)
    ahead[1, :, :, 1] = split_planes(cosine)
    ahead = ahead.reshape(2 * NG, 2 * NG)
    return np.concatenate([ahead, ahead.T], 0)


@functools.lru_cache(None)
def mask_rounds():
    edges = {source: [] for source in range(N_FFT)}
    for device in range(N_FFT):
        for rows in range(4):
            index = KY[rows][device] % NG
            edges[index // SLAB].append((device, index % SLAB, rows))
    rounds = []
    for _ in range(SLAB):
        taken = {}

        def place(source, seen):
            for edge in edges[source]:
                if edge[0] in seen:
                    continue
                seen.add(edge[0])
                if edge[0] not in taken or place(taken[edge[0]][0], seen):
                    taken[edge[0]] = (source, edge)
                    return True
            return False

        for source in range(N_FFT):
            assert place(source, set())
        pairs, local, slot = [], [0] * N_FFT, [0] * N_FFT
        for device, (source, edge) in taken.items():
            edges[source].remove(edge)
            pairs.append((source, device))
            local[source] = edge[1]
            slot[device] = edge[2]
        rounds.append((tuple(sorted(pairs)), tuple(local), tuple(slot)))
    return tuple(rounds)


@functools.lru_cache(None)
def device_table():
    out = np.zeros((N_FFT, 16), np.int32)
    for turn_, (_, local, slot) in enumerate(mask_rounds()):
        for device in range(N_FFT):
            ky = KY[slot[device]][device]
            out[device, turn_] = local[device]
            out[device, 4 + turn_] = kept(ky)
            out[device, 8 + turn_] = ky
            out[device, 12 + turn_] = slot[device]
    return out.reshape(-1)


ZERO_ROUND = [slot[0] for _, _, slot in mask_rounds()].index(0)


@functools.lru_cache(None)
def shared_width():
    width = np.repeat(np.asarray([kept(k) for k in KY[2]], np.int32), BLOCK)
    return np.ascontiguousarray(np.broadcast_to(width[:, None], (2 * NG, LANES)))


def split(value):
    high = value.astype(jnp.bfloat16)
    return high, (value - high.astype(jnp.float32)).astype(jnp.bfloat16)


def dot(left, right):
    return jnp.dot(left, right, preferred_element_type=jnp.float32)


def dot3(left, right):
    return dot(left[0], right[0]) + (dot(left[1], right[0]) + dot(left[0], right[1]))


def both(ref, start=0, size=None):
    size = ref.shape[1] if size is None else size
    return ref[0, start : start + size, :], ref[1, start : start + size, :]


def lane_roll(value, shift):
    shift %= LANES
    return value if shift == 0 else pltpu.roll(value, shift, 1)


def parts_swapped(value):
    blocks = value.reshape(-1, BLOCK, value.shape[1])
    return pltpu.roll(blocks, SLAB, 1).reshape(value.shape)


def beside(parts):
    return parts[0] if len(parts) == 1 else jnp.concatenate(parts, axis=1)


def iota(shape, dim):
    return lax.broadcasted_iota(jnp.int32, shape, dim)


def ahead_body(count, products_of, n_in, *refs):
    inputs = refs[:n_in]
    y_ref, z_ref, width_ref, out_ref, *grids = refs[n_in:]
    pieces, size = layout(count)
    fields = products_of(inputs)
    is_imag = iota((2 * NG, LANES), 0) % BLOCK >= SLAB
    sides = {}
    table = both(y_ref)
    for first in range(0, count, 2):
        two = range(first, min(first + 2, count))
        for x in range(SLAB):
            plane = slice(NG * x, NG * x + NG)
            cells = [fields[field](plane) for field in two]
            lines = dot3(table, split(beside(cells)))
            for spot, field in enumerate(two):
                piece = lines[:, NG * spot : NG * (spot + 1)]
                grids[field][pl.ds(x, 2 * NG, stride=SLAB), :] = piece
        for rows in range(4):
            block = slice(2 * NG * rows, 2 * NG * (rows + 1))
            lines = split(beside([grids[field][block, :] for field in two]))
            lines = dot3(lines, both(z_ref, 2 * NG if rows == 3 else 0, NG * len(two)))
            turned = parts_swapped(lines[:, LANES:])
            sides[first // 2, rows] = lines[:, :LANES] + jnp.where(is_imag, -turned, turned)
    lane = iota((2 * NG, LANES), 1)
    shared = {}
    for field in range(count):
        shift = HALF * (field % 2)
        wide = lane_roll(sides[field // 2, 2], -shift)
        narrow = lane_roll(sides[field // 2, 3], SHARED - HALF - shift)
        shared[field] = jnp.where(lane < width_ref[...], wide, narrow)
    tiles = [None] * (size // LANES)
    for kind, field, first, lanes, place in pieces:
        if kind == 2:
            value, shift = shared[field], 0
        else:
            value, shift = sides[field // 2, kind], HALF * (field % 2)
        start = place % LANES
        value = lane_roll(value, start - first - shift)
        old = tiles[place // LANES]
        if old is None:
            old = jnp.zeros_like(value)
        tiles[place // LANES] = jnp.where((lane >= start) & (lane < start + lanes), value, old)
    for tile, value in enumerate(tiles):
        out_ref[:, LANES * tile : LANES * (tile + 1)] = value
    row, column = iota((BLOCK, LANES), 0), iota((BLOCK, LANES), 1)
    sign = (1 - 2 * (iota((1, NG), 1) % 2)).astype(jnp.float32)
    for kind, field, _, _, place in pieces:
        if kind:
            continue
        extra = jnp.zeros((BLOCK, LANES), jnp.float32)
        for x in range(SLAB):
            cells = fields[field](slice(NG * x, NG * x + NG))
            cells = jnp.sum(cells, axis=0, keepdims=True) * sign
            value = jnp.sum(cells, axis=1, keepdims=True)
            extra = jnp.where((row == SLAB + x) & (column == place % LANES), value, extra)
        tile = place // LANES * LANES
        out_ref[0:BLOCK, tile : tile + LANES] += extra


def middle_body(me_ref, device_ref, x_ref, lane_ref, table_ref, *rest):
    *mask_refs, out_ref = rest
    size = x_ref.shape[1]
    base = me_ref[0] * 16
    masks = [ref[...].astype(jnp.float32).astype(jnp.bfloat16) for ref in mask_refs]
    zero_mask = mask_refs[ZERO_ROUND][0:1, HALF : HALF + 1].astype(jnp.float32)
    is_imag = iota((2 * NG, LANES), 0) % BLOCK >= SLAB
    kx = iota((NG, LANES), 0)
    signed = jnp.where(kx < HALF, kx, kx - NG)
    forward = both(table_ref, 0, 2 * NG)
    inverse = both(table_ref, 2 * NG, 2 * NG)
    special = zero_mask / ((1.0 + HALF * HALF / (NG * NG / 16.0)) * float(NG**3))
    for step in range(0, size, 2 * LANES):
        values, real, imag = [], [], []
        for start in range(step, min(step + 2 * LANES, size), LANES):
            lanes = slice(start, start + LANES)
            value = x_ref[:, lanes]
            zero = (lane_ref[0:1, lanes] == 0) & (me_ref[0] == 0)
            mean = jnp.sum(jnp.where(is_imag, value, 0.0), axis=0, keepdims=True) * (1.0 / NG)
            values.append(jnp.where(is_imag & zero, mean, value))
            cells = jnp.zeros((NG, LANES), jnp.float32)
            squared = jnp.zeros((1, LANES), jnp.int32)
            for turn_ in range(4):
                slot = device_ref[base + 12 + turn_]
                kz = lane_ref[0:1, lanes]
                for which in range(1, 4):
                    kz = jnp.where(slot == which, lane_ref[which : which + 1, lanes], kz)
                ky = device_ref[base + 8 + turn_]
                chosen = kz < device_ref[base + 4 + turn_]
                spread = jnp.where((kx == kz) & chosen, 1.0, 0.0).astype(jnp.bfloat16)
                cells += dot(masks[turn_], spread)
                squared += jnp.where(chosen, kz * kz + ky * ky, 0)
            squared = (signed * signed + squared).astype(jnp.float32)
            weight = cells / ((1.0 + squared / (NG * NG / 16.0)) * float(NG**3))
            real.append(weight)
            imag.append(jnp.where((kx == 0) & zero, special, weight))
        spectrum = dot3(forward, split(beside(values)))
        weight = jnp.concatenate([beside(real), beside(imag)], axis=0)
        width = LANES * len(values)
        out_ref[:, step : step + width] = dot3(inverse, split(spectrum * weight))


def potentials(count, lines_ref, y_ref, z_ref, width_ref, grids):
    pieces, _ = layout(count)
    lane = iota((2 * NG, LANES), 1)
    is_imag = iota((2 * NG, LANES), 0) % BLOCK >= SLAB
    sides = {}

    def add(key, value):
        sides[key] = value if key not in sides else sides[key] + value

    shared = {}
    for kind, field, first, lanes, place in pieces:
        tile = place // LANES * LANES
        start = place % LANES
        value = lines_ref[:, tile : tile + LANES]
        value = jnp.where((lane >= start) & (lane < start + lanes), value, 0.0)
        shift = first - start
        if kind == 2:
            value = lane_roll(value, shift)
            shared[field] = value if field not in shared else shared[field] + value
        else:
            add((field // 2, kind), lane_roll(value, shift + HALF * (field % 2)))
    for field, value in shared.items():
        shift = HALF * (field % 2)
        wide = lane < width_ref[...]
        add((field // 2, 2), lane_roll(jnp.where(wide, value, 0.0), shift))
        add((field // 2, 3), lane_roll(jnp.where(wide, 0.0, value), HALF - SHARED + shift))
    for (index, rows), value in sides.items():
        turned = parts_swapped(value)
        value = jnp.concatenate([value, jnp.where(is_imag, turned, -turned)], axis=1)
        table = both(z_ref, 2 * NG if rows == 3 else 0, 2 * NG)
        cells = dot3(split(value), table)
        for field in range(2 * index, min(2 * index + 2, count)):
            block = slice(2 * NG * rows, 2 * NG * (rows + 1))
            grids[field][block, :] = cells[:, NG * (field % 2) : NG * (field % 2 + 1)]
    table = both(y_ref)

    def plane_of(x):
        out = []
        for first in range(0, count, 2):
            two = grids[first : first + 2]
            lines = beside([ref[pl.ds(x, 2 * NG, stride=SLAB), :] for ref in two])
            cells = dot3(table, split(lines))
            out += [cells[:, NG * spot : NG * (spot + 1)] for spot in range(len(two))]
        return out

    return plane_of


def back_own_body(own_ref, lines_ref, y_ref, z_ref, width_ref, out_ref, *grids):
    plane_of = potentials(3, lines_ref, y_ref, z_ref, width_ref, grids)
    for x in range(SLAB):
        plane = slice(NG * x, NG * x + NG)
        first, mixed, second = plane_of(x)
        out_ref[0, plane, :] = first * own_ref[0, plane, :] + mixed * own_ref[1, plane, :]
        out_ref[1, plane, :] = mixed * own_ref[0, plane, :] + second * own_ref[1, plane, :]


def back_cross_body(other_ref, sum_ref, lines_ref, y_ref, z_ref, width_ref, out_ref, *grids):
    plane_of = potentials(4, lines_ref, y_ref, z_ref, width_ref, grids)
    for x in range(SLAB):
        plane = slice(NG * x, NG * x + NG)
        cells = plane_of(x)
        for band in range(2):
            total = cells[2 * band] * other_ref[0, plane, :]
            total += cells[2 * band + 1] * other_ref[1, plane, :]
            out_ref[band, plane, :] = -0.5 * (sum_ref[band, plane, :] + total)


def product(left, i, right, j):
    return lambda plane: left[i, plane, :] * right[j, plane, :]


def own_products(refs):
    (own,) = refs
    return [product(own, 0, own, 0), product(own, 0, own, 1), product(own, 1, own, 1)]


def cross_products(refs):
    own, other = refs
    return [product(own, b, other, j) for b in range(2) for j in range(2)]


def mask_body(me_ref, device_ref, mask_ref, *out_refs):
    for turn_, out_ref in enumerate(out_refs):
        row = device_ref[me_ref[0] * 16 + turn_]
        out_ref[...] = mask_ref[pl.ds(row, NG, stride=SLAB), :]


def params():
    return pltpu.CompilerParams(vmem_limit_bytes=VMEM_LIMIT)


def cost(flops, moved):
    return pl.CostEstimate(flops=flops, bytes_accessed=moved, transcendentals=0)


def call(body, shape, args, fields, name):
    return pl.pallas_call(
        body,
        out_shape=jax.ShapeDtypeStruct(shape, jnp.float32),
        in_specs=[pl.BlockSpec(memory_space=pltpu.VMEM) for _ in args],
        out_specs=pl.BlockSpec(memory_space=pltpu.VMEM),
        scratch_shapes=[pltpu.VMEM((ROWS_ALL, NG), jnp.float32) for _ in range(fields)],
        compiler_params=params(),
        cost_estimate=cost(5 * 10**9, 4 * 10**6),
        name=name,
    )(*args)


def ahead(count, products_of, grids, name):
    tables = (pair(y_table()), pair(z_ahead()), shared_width())
    args = [*grids, *(jnp.asarray(table) for table in tables)]
    body = functools.partial(ahead_body, count, products_of, len(grids))
    return call(body, (2 * NG, layout(count)[1]), args, count, name)


def back(body, count, grids, values, name):
    tables = (pair(y_table().T), pair(z_back()), shared_width())
    args = [*grids, values, *(jnp.asarray(table) for table in tables)]
    return call(body, (2, SLAB * NG, NG), args, count, name)


def indexed(body, shapes, args, me, flops, name):
    vmem = lambda: pl.BlockSpec(memory_space=pltpu.VMEM)
    return pl.pallas_call(
        body,
        out_shape=shapes,
        grid_spec=pltpu.PrefetchScalarGridSpec(
            num_scalar_prefetch=2,
            grid=(),
            in_specs=[vmem() for _ in args],
            out_specs=[vmem() for _ in shapes],
        ),
        compiler_params=params(),
        cost_estimate=cost(flops, 2 * 10**6),
        name=name,
    )(me, jnp.asarray(device_table()), *args)


def middle(count, values, masks, me, name):
    args = [values, jnp.asarray(lane_rows(count)), jnp.asarray(pair(x_tables())), *masks]
    shape = jax.ShapeDtypeStruct(values.shape, jnp.float32)
    return indexed(middle_body, [shape], args, me, 2 * 10**9, name)[0]


def mask_rows(mask, me):
    shapes = [jax.ShapeDtypeStruct((NG, NG), jnp.int32)] * SLAB
    return indexed(mask_body, shapes, [mask.reshape(NG * SLAB, NG)], me, 10**6, "mask_rows")


def swap(values):
    size = values.shape[1]
    blocks = values.reshape(N_FFT, BLOCK, size)
    blocks = lax.all_to_all(blocks, "fft", split_axis=0, concat_axis=0, tiled=True)
    return blocks.reshape(2 * NG, size)


def body(orbitals, mask):
    me = lax.axis_index("fft").astype(jnp.int32)[None]
    count = lax.axis_size("band")
    other = lax.ppermute(orbitals, "band", [(i, (i + 1) % count) for i in range(count)])
    own = orbitals.reshape(2, SLAB * NG, NG)
    other = other.reshape(2, SLAB * NG, NG)

    sent_own = ahead(3, own_products, (own,), "ahead_own")
    sent_own, mask = lax.optimization_barrier((sent_own, mask))
    lines_own = swap(sent_own)
    masks = [
        lax.ppermute(rows, "fft", pairs)
        for rows, (pairs, _, _) in zip(mask_rows(mask, me), mask_rounds())
    ]
    other, masks = lax.optimization_barrier((other, masks))
    lines_cross = swap(ahead(4, cross_products, (own, other), "ahead_cross"))
    lines_own = swap(middle(3, lines_own, masks, me, "middle_own"))
    lines_cross = swap(middle(4, lines_cross, masks, me, "middle_cross"))
    total = back(back_own_body, 3, (own,), lines_own, "back_own")
    total = back(back_cross_body, 4, (other, total), lines_cross, "back_cross")
    return total.reshape(orbitals.shape)


def solution(mesh):
    in_specs = (P("band", "fft", None, None), P(None, "fft", None))
    out_specs = P("band", "fft", None, None)
    return jax.shard_map(body, mesh=mesh, in_specs=in_specs, out_specs=out_specs, check_vma=False)
```

```python
import functools
import math

import jax
import jax.numpy as jnp
import ml_dtypes
import numpy as np
from jax import lax
from jax.experimental import pallas as pl
from jax.experimental.pallas import tpu as pltpu
from jax.sharding import PartitionSpec as P

NG = 128
HALF = NG // 2
N_FFT = 32
SLAB = NG // N_FFT
BLOCK = 2 * SLAB
LANES = 128
ROWS_ALL = 4 * 2 * NG
NO_LINE = 999
VMEM_LIMIT = 20 * 1024 * 1024
VMEM_MOST = 56 * 1024 * 1024


def kept(ky):
    return min(HALF, math.isqrt(HALF * HALF - ky * ky) + 1)


def row_sets():
    order = sorted(range(-HALF, HALF), key=lambda k: (abs(k), -k))
    return [order[:32], order[32:64], order[64:96], order[:95:-1]]


KY = row_sets()
WIDE = [max(kept(k) for k in KY[0]), max(kept(k) for k in KY[1])]
SHARED = max(kept(a) + kept(b) for a, b in zip(KY[2], KY[3]))


def layout(count):
    if count == 3:
        rest = NG // 2 - WIDE[1]
        tail = 3 * SHARED - 2 * LANES
        assert 0 <= tail <= rest
        pieces = [(0, f, 0, WIDE[0], HALF * f) for f in range(3)]
        pieces += [(1, 2, 0, WIDE[1], 3 * HALF), (2, 2, SHARED - tail, tail, 3 * HALF + WIDE[1])]
        pieces += [(1, f, 0, WIDE[1], 4 * HALF + HALF * f) for f in range(2)]
        start = 6 * HALF
        pieces += [(2, f, 0, SHARED - (tail if f == 2 else 0), start + SHARED * f) for f in range(3)]
        size = start + 2 * LANES
    else:
        pieces = [(0, f, 0, WIDE[0], HALF * f) for f in range(4)]
        pieces += [(1, f, 0, WIDE[1], HALF * (4 + f)) for f in range(4)]
        pieces += [(2, f, 0, SHARED, 8 * HALF + 96 * f) for f in range(4)]
        size = 7 * LANES
    cut = []
    for kind, field, first, lanes, place in pieces:
        while lanes:
            step = min(lanes, LANES - place % LANES)
            cut.append((kind, field, first, step, place))
            first, lanes, place = first + step, lanes - step, place + step
    return cut, size


@functools.lru_cache(None)
def lane_rows(count):
    pieces, size = layout(count)
    out = np.full((8, size), NO_LINE, np.int32)
    for kind, _, first, lanes, place in pieces:
        spots = np.arange(lanes)
        out[kind, place + spots] = first + spots
        if kind == 2:
            out[3, place + spots] = SHARED - 1 - first - spots
    return out


def turn(a, b):
    angle = (np.asarray(a)[:, None] * np.asarray(b)[None, :]) % NG * (2.0 * np.pi / NG)
    return np.cos(angle), np.sin(angle)


def pair(table):
    high = table.astype(np.float32).astype(ml_dtypes.bfloat16)
    low = (table - high.astype(np.float64)).astype(np.float32).astype(ml_dtypes.bfloat16)
    return np.stack([high, low])


POINTS = np.arange(NG)


@functools.lru_cache(None)
def y_table():
    cosine, sine = turn(np.concatenate(KY), POINTS)
    return np.stack([cosine, -sine], 1).reshape(2 * NG, NG)


def doubled(block):
    return np.kron(np.eye(2), block)


@functools.lru_cache(None)
def z_ahead():
    out = []
    for kz in (np.arange(HALF), np.arange(HALF)[::-1]):
        cosine, sine = turn(POINTS, kz)
        out.append(np.concatenate([doubled(cosine), doubled(sine)], 1))
    return np.concatenate(out, 0)


@functools.lru_cache(None)
def z_back():
    out = []
    for kz in (np.arange(HALF), np.arange(HALF)[::-1]):
        cosine, sine = turn(kz, POINTS)
        weight = np.where(kz == 0, 1.0, 2.0)[:, None]
        cosine, sine = weight * cosine, weight * sine
        sine[kz == 0] = -(1.0 - 2.0 * (POINTS % 2))
        out.append(np.concatenate([doubled(cosine), doubled(sine)], 0))
    return np.concatenate(out, 0)


@functools.lru_cache(None)
def x_tables():
    cosine, sine = turn(POINTS, POINTS)
    ahead = np.zeros((2, NG, N_FFT, 2, SLAB))
    split_planes = lambda table: table.reshape(NG, N_FFT, SLAB)
    ahead[0, :, :, 0] = split_planes(cosine)
    ahead[0, :, :, 1] = split_planes(sine)
    ahead[1, :, :, 0] = split_planes(-sine)
    ahead[1, :, :, 1] = split_planes(cosine)
    ahead = ahead.reshape(2 * NG, 2 * NG)
    return np.concatenate([ahead, ahead.T], 0)


@functools.lru_cache(None)
def mask_rounds():
    edges = {source: [] for source in range(N_FFT)}
    for device in range(N_FFT):
        for rows in range(4):
            index = KY[rows][device] % NG
            edges[index // SLAB].append((device, index % SLAB, rows))
    rounds = []
    for _ in range(SLAB):
        taken = {}

        def place(source, seen):
            for edge in edges[source]:
                if edge[0] in seen:
                    continue
                seen.add(edge[0])
                if edge[0] not in taken or place(taken[edge[0]][0], seen):
                    taken[edge[0]] = (source, edge)
                    return True
            return False

        for source in range(N_FFT):
            assert place(source, set())
        pairs, local, slot = [], [0] * N_FFT, [0] * N_FFT
        for device, (source, edge) in taken.items():
            edges[source].remove(edge)
            pairs.append((source, device))
            local[source] = edge[1]
            slot[device] = edge[2]
        rounds.append((tuple(sorted(pairs)), tuple(local), tuple(slot)))
    return tuple(rounds)


@functools.lru_cache(None)
def device_table():
    out = np.zeros((N_FFT, 16), np.int32)
    for turn_, (_, local, slot) in enumerate(mask_rounds()):
        for device in range(N_FFT):
            ky = KY[slot[device]][device]
            out[device, turn_] = local[device]
            out[device, 4 + turn_] = kept(ky)
            out[device, 8 + turn_] = ky
            out[device, 12 + turn_] = slot[device]
    return out.reshape(-1)


ZERO_ROUND = [slot[0] for _, _, slot in mask_rounds()].index(0)


@functools.lru_cache(None)
def shared_width():
    width = np.repeat(np.asarray([kept(k) for k in KY[2]], np.int32), BLOCK)
    return np.ascontiguousarray(np.broadcast_to(width[:, None], (2 * NG, LANES)))


def split(value):
    high = value.astype(jnp.bfloat16)
    return high, (value - high.astype(jnp.float32)).astype(jnp.bfloat16)


def dot(left, right):
    return jnp.dot(left, right, preferred_element_type=jnp.float32)


def dot3(left, right):
    return dot(left[0], right[0]) + (dot(left[1], right[0]) + dot(left[0], right[1]))


def both(ref, start=0, size=None):
    size = ref.shape[1] if size is None else size
    return ref[0, start : start + size, :], ref[1, start : start + size, :]


def lane_roll(value, shift):
    shift %= LANES
    return value if shift == 0 else pltpu.roll(value, shift, 1)


def parts_swapped(value):
    blocks = value.reshape(-1, BLOCK, value.shape[1])
    return pltpu.roll(blocks, SLAB, 1).reshape(value.shape)


def beside(parts):
    return parts[0] if len(parts) == 1 else jnp.concatenate(parts, axis=1)


def iota(shape, dim):
    return lax.broadcasted_iota(jnp.int32, shape, dim)


def ahead_body(count, products_of, n_in, *refs):
    inputs = refs[:n_in]
    y_ref, z_ref, width_ref, out_ref, *grids = refs[n_in:]
    pieces, size = layout(count)
    fields = products_of(inputs)
    is_imag = iota((2 * NG, LANES), 0) % BLOCK >= SLAB
    sides = {}
    table = both(y_ref)
    for first in range(0, count, 2):
        two = range(first, min(first + 2, count))
        for x in range(SLAB):
            plane = slice(NG * x, NG * x + NG)
            cells = [fields[field](plane) for field in two]
            lines = dot3(table, split(beside(cells)))
            for spot, field in enumerate(two):
                piece = lines[:, NG * spot : NG * (spot + 1)]
                grids[field][pl.ds(x, 2 * NG, stride=SLAB), :] = piece
        for rows in range(4):
            block = slice(2 * NG * rows, 2 * NG * (rows + 1))
            lines = split(beside([grids[field][block, :] for field in two]))
            lines = dot3(lines, both(z_ref, 2 * NG if rows == 3 else 0, NG * len(two)))
            turned = parts_swapped(lines[:, LANES:])
            sides[first // 2, rows] = lines[:, :LANES] + jnp.where(is_imag, -turned, turned)
    lane = iota((2 * NG, LANES), 1)
    shared = {}
    for field in range(count):
        shift = HALF * (field % 2)
        wide = lane_roll(sides[field // 2, 2], -shift)
        narrow = lane_roll(sides[field // 2, 3], SHARED - HALF - shift)
        shared[field] = jnp.where(lane < width_ref[...], wide, narrow)
    tiles = [None] * (size // LANES)
    for kind, field, first, lanes, place in pieces:
        if kind == 2:
            value, shift = shared[field], 0
        else:
            value, shift = sides[field // 2, kind], HALF * (field % 2)
        start = place % LANES
        value = lane_roll(value, start - first - shift)
        old = tiles[place // LANES]
        if old is None:
            old = jnp.zeros_like(value)
        tiles[place // LANES] = jnp.where((lane >= start) & (lane < start + lanes), value, old)
    for tile, value in enumerate(tiles):
        out_ref[:, LANES * tile : LANES * (tile + 1)] = value
    row, column = iota((BLOCK, LANES), 0), iota((BLOCK, LANES), 1)
    sign = (1 - 2 * (iota((1, NG), 1) % 2)).astype(jnp.float32)
    for kind, field, _, _, place in pieces:
        if kind:
            continue
        extra = jnp.zeros((BLOCK, LANES), jnp.float32)
        for x in range(SLAB):
            cells = fields[field](slice(NG * x, NG * x + NG))
            cells = jnp.sum(cells, axis=0, keepdims=True) * sign
            value = jnp.sum(cells, axis=1, keepdims=True)
            extra = jnp.where((row == SLAB + x) & (column == place % LANES), value, extra)
        tile = place // LANES * LANES
        out_ref[0:BLOCK, tile : tile + LANES] += extra


def middle_body(me_ref, device_ref, x_ref, lane_ref, table_ref, *rest):
    *mask_refs, out_ref, done = rest
    size = x_ref.shape[1]
    before = out_ref.shape[1] - size
    if before:
        ready_ref, *mask_refs = mask_refs
        copy = pltpu.make_async_copy(ready_ref, out_ref.at[:, :before], done)
        copy.start()
    base = me_ref[0] * 16
    spot = (iota((HALF, LANES), 0) == 0) & (iota((HALF, LANES), 1) == HALF - 1)
    masks = []
    for ref in mask_refs:
        cells = ref[...].astype(jnp.float32)
        high = jnp.where(spot, 0.0, pltpu.roll(cells, HALF, 1))
        masks.append(jnp.concatenate([cells, high], axis=0).astype(jnp.bfloat16))
    zero_mask = mask_refs[ZERO_ROUND][0:1, LANES - 1 : LANES].astype(jnp.float32)
    is_imag = iota((2 * NG, LANES), 0) % BLOCK >= SLAB
    kx = iota((NG, LANES), 0)
    signed = jnp.where(kx < HALF, kx, kx - NG)
    forward = both(table_ref, 0, 2 * NG)
    inverse = both(table_ref, 2 * NG, 2 * NG)
    special = zero_mask / ((1.0 + HALF * HALF / (NG * NG / 16.0)) * float(NG**3))
    for step in range(0, size, 2 * LANES):
        values, real, imag = [], [], []
        for start in range(step, min(step + 2 * LANES, size), LANES):
            lanes = slice(start, start + LANES)
            value = x_ref[:, lanes]
            zero = (lane_ref[0:1, lanes] == 0) & (me_ref[0] == 0)
            mean = jnp.sum(jnp.where(is_imag, value, 0.0), axis=0, keepdims=True) * (1.0 / NG)
            values.append(jnp.where(is_imag & zero, mean, value))
            cells = jnp.zeros((NG, LANES), jnp.float32)
            squared = jnp.zeros((1, LANES), jnp.int32)
            for turn_ in range(4):
                slot = device_ref[base + 12 + turn_]
                kz = lane_ref[0:1, lanes]
                for which in range(1, 4):
                    kz = jnp.where(slot == which, lane_ref[which : which + 1, lanes], kz)
                ky = device_ref[base + 8 + turn_]
                chosen = kz < device_ref[base + 4 + turn_]
                spread = jnp.where((kx == kz) & chosen, 1.0, 0.0).astype(jnp.bfloat16)
                cells += dot(masks[turn_], spread)
                squared += jnp.where(chosen, kz * kz + ky * ky, 0)
            squared = (signed * signed + squared).astype(jnp.float32)
            weight = cells / ((1.0 + squared / (NG * NG / 16.0)) * float(NG**3))
            real.append(weight)
            imag.append(jnp.where((kx == 0) & zero, special, weight))
        spectrum = dot3(forward, split(beside(values)))
        weight = jnp.concatenate([beside(real), beside(imag)], axis=0)
        width = LANES * len(values)
        out_ref[:, before + step : before + step + width] = dot3(inverse, split(spectrum * weight))
    if before:
        copy.wait()


def potentials(count, offset, lines_ref, y_ref, z_ref, width_ref, grids):
    pieces, _ = layout(count)
    pieces = [(*piece[:4], piece[4] + offset) for piece in pieces]
    lane = iota((2 * NG, LANES), 1)
    is_imag = iota((2 * NG, LANES), 0) % BLOCK >= SLAB
    sides = {}

    def add(key, value):
        sides[key] = value if key not in sides else sides[key] + value

    shared = {}
    for kind, field, first, lanes, place in pieces:
        tile = place // LANES * LANES
        start = place % LANES
        value = lines_ref[:, tile : tile + LANES]
        value = jnp.where((lane >= start) & (lane < start + lanes), value, 0.0)
        shift = first - start
        if kind == 2:
            value = lane_roll(value, shift)
            shared[field] = value if field not in shared else shared[field] + value
        else:
            add((field // 2, kind), lane_roll(value, shift + HALF * (field % 2)))
    for field, value in shared.items():
        shift = HALF * (field % 2)
        wide = lane < width_ref[...]
        add((field // 2, 2), lane_roll(jnp.where(wide, value, 0.0), shift))
        add((field // 2, 3), lane_roll(jnp.where(wide, 0.0, value), HALF - SHARED + shift))
    for (index, rows), value in sides.items():
        turned = parts_swapped(value)
        value = jnp.concatenate([value, jnp.where(is_imag, turned, -turned)], axis=1)
        table = both(z_ref, 2 * NG if rows == 3 else 0, 2 * NG)
        cells = dot3(split(value), table)
        for field in range(2 * index, min(2 * index + 2, count)):
            block = slice(2 * NG * rows, 2 * NG * (rows + 1))
            grids[field][block, :] = cells[:, NG * (field % 2) : NG * (field % 2 + 1)]
    table = both(y_ref)

    def plane_of(x):
        out = []
        for first in range(0, count, 2):
            two = grids[first : first + 2]
            lines = beside([ref[pl.ds(x, 2 * NG, stride=SLAB), :] for ref in two])
            cells = dot3(table, split(lines))
            out += [cells[:, NG * spot : NG * (spot + 1)] for spot in range(len(two))]
        return out

    return plane_of


def back_body(own_ref, other_ref, lines_ref, y_ref, z_ref, width_ref, out_ref, *grids):
    tables = (lines_ref, y_ref, z_ref, width_ref)
    own_plane = potentials(3, 0, *tables, grids[:3])
    cross_plane = potentials(4, layout(3)[1], *tables, grids[3:])
    for x in range(SLAB):
        plane = slice(NG * x, NG * x + NG)
        own = [own_ref[band, plane, :] for band in range(2)]
        other = [other_ref[band, plane, :] for band in range(2)]
        first, mixed, second = own_plane(x)
        cross = cross_plane(x)
        total = first * own[0] + mixed * own[1] + (cross[0] * other[0] + cross[1] * other[1])
        out_ref[0, plane, :] = -0.5 * total
        total = mixed * own[0] + second * own[1] + (cross[2] * other[0] + cross[3] * other[1])
        out_ref[1, plane, :] = -0.5 * total


def product(left, i, right, j):
    return lambda plane: left[i, plane, :] * right[j, plane, :]


def own_products(refs):
    (own,) = refs
    return [product(own, 0, own, 0), product(own, 0, own, 1), product(own, 1, own, 1)]


def cross_products(refs):
    own, other = refs
    return [product(own, b, other, j) for b in range(2) for j in range(2)]


def mask_body(me_ref, device_ref, mask_ref, *out_refs):
    lane = iota((HALF, LANES), 1)
    for turn_, out_ref in enumerate(out_refs):
        row = device_ref[me_ref[0] * 16 + turn_]
        low = mask_ref[pl.ds(row, HALF, stride=SLAB), :]
        high = mask_ref[pl.ds(row + HALF * SLAB, HALF, stride=SLAB), :]
        packed = jnp.where(lane < HALF, low, pltpu.roll(high, HALF, 1))
        spot = (iota((HALF, LANES), 0) == 0) & (lane == LANES - 1)
        out_ref[...] = jnp.where(spot, low[0:1, HALF : HALF + 1], packed)


def params(limit=VMEM_LIMIT):
    return pltpu.CompilerParams(vmem_limit_bytes=limit)


def cost(flops, moved):
    return pl.CostEstimate(flops=flops, bytes_accessed=moved, transcendentals=0)


def call(body, shape, args, fields, flops, limit, name):
    return pl.pallas_call(
        body,
        out_shape=jax.ShapeDtypeStruct(shape, jnp.float32),
        in_specs=[pl.BlockSpec(memory_space=pltpu.VMEM) for _ in args],
        out_specs=pl.BlockSpec(memory_space=pltpu.VMEM),
        scratch_shapes=[pltpu.VMEM((ROWS_ALL, NG), jnp.float32) for _ in range(fields)],
        compiler_params=params(limit),
        cost_estimate=cost(flops, 4 * 10**6),
        name=name,
    )(*args)


def ahead(count, products_of, grids, flops, limit, name):
    tables = (pair(y_table()), pair(z_ahead()), shared_width())
    args = [*grids, *(jnp.asarray(table) for table in tables)]
    body = functools.partial(ahead_body, count, products_of, len(grids))
    return call(body, (2 * NG, layout(count)[1]), args, count, flops, limit, name)


def back(own, other, values):
    tables = (pair(y_table().T), pair(z_back()), shared_width())
    args = [own, other, values, *(jnp.asarray(table) for table in tables)]
    return call(back_body, (2, SLAB * NG, NG), args, 7, 5 * 10**9, VMEM_LIMIT, "back")


def indexed(body, shapes, args, me, flops, name, scratch=(), away=()):
    vmem = lambda: pl.BlockSpec(memory_space=pltpu.VMEM)
    return pl.pallas_call(
        body,
        out_shape=shapes,
        grid_spec=pltpu.PrefetchScalarGridSpec(
            num_scalar_prefetch=2,
            grid=(),
            in_specs=[
                pl.BlockSpec(memory_space=pl.ANY) if spot in away else vmem()
                for spot in range(len(args))
            ],
            out_specs=[vmem() for _ in shapes],
            scratch_shapes=list(scratch),
        ),
        compiler_params=params(),
        cost_estimate=cost(flops, 2 * 10**6),
        name=name,
    )(me, jnp.asarray(device_table()), *args)


def middle(count, values, ready, masks, me, name):
    args = [values, jnp.asarray(lane_rows(count)), jnp.asarray(pair(x_tables())), *ready, *masks]
    size = values.shape[1] + sum(part.shape[1] for part in ready)
    shape = jax.ShapeDtypeStruct((2 * NG, size), jnp.float32)
    scratch, away = [pltpu.SemaphoreType.DMA], [3] if ready else []
    return indexed(middle_body, [shape], args, me, 2 * 10**9, name, scratch, away)[0]


def mask_rows(mask, me):
    shapes = [jax.ShapeDtypeStruct((HALF, NG), jnp.int32)] * SLAB
    return indexed(mask_body, shapes, [mask.reshape(NG * SLAB, NG)], me, 10**6, "mask_rows")


def swap(values):
    size = values.shape[1]
    blocks = values.reshape(N_FFT, BLOCK, size)
    blocks = lax.all_to_all(blocks, "fft", split_axis=0, concat_axis=0, tiled=True)
    return blocks.reshape(2 * NG, size)


def body(orbitals, mask):
    me = lax.axis_index("fft").astype(jnp.int32)[None]
    count = lax.axis_size("band")
    other = lax.ppermute(orbitals, "band", [(i, (i + 1) % count) for i in range(count)])
    own = orbitals.reshape(2, SLAB * NG, NG)
    other = other.reshape(2, SLAB * NG, NG)

    sent_own = ahead(3, own_products, (own,), 2 * 10**10, VMEM_MOST, "ahead_own")
    sent_own, mask = lax.optimization_barrier((sent_own, mask))
    lines_own = swap(sent_own)
    masks = [
        lax.ppermute(rows, "fft", pairs)
        for rows, (pairs, _, _) in zip(mask_rows(mask, me), mask_rounds())
    ]
    sent_cross = ahead(4, cross_products, (own, other), 2 * 10**10, VMEM_LIMIT, "ahead_cross")
    (sent_cross, masks[0], masks[1]) = lax.optimization_barrier((sent_cross, masks[0], masks[1]))
    lines_cross = swap(sent_cross)
    lines_own = middle(3, lines_own, [], masks, me, "middle_own")
    lines = swap(middle(4, lines_cross, [lines_own], masks, me, "middle_cross"))
    return back(own, other, lines).reshape(orbitals.shape)


def solution(mesh):
    in_specs = (P("band", "fft", None, None), P(None, "fft", None))
    out_specs = P("band", "fft", None, None)
    return jax.shard_map(body, mesh=mesh, in_specs=in_specs, out_specs=out_specs, check_vma=False)
```

```python
import functools
import math

import jax
import jax.numpy as jnp
import ml_dtypes
import numpy as np
from jax import lax
from jax.experimental import pallas as pl
from jax.experimental.pallas import tpu as pltpu
from jax.sharding import PartitionSpec as P

NG = 128
HALF = NG // 2
N_FFT = 32
SLAB = NG // N_FFT
BLOCK = 2 * SLAB
LANES = 128
ROWS_ALL = 4 * 2 * NG
NO_LINE = 999
VMEM_LIMIT = 20 * 1024 * 1024
VMEM_MOST = 56 * 1024 * 1024


def kept(ky):
    return min(HALF, math.isqrt(HALF * HALF - ky * ky) + 1)


def row_sets():
    order = sorted(range(-HALF, HALF), key=lambda k: (abs(k), -k))
    return [order[:32], order[32:64], order[64:96], order[:95:-1]]


KY = row_sets()
WIDE = [max(kept(k) for k in KY[0]), max(kept(k) for k in KY[1])]
SHARED = max(kept(a) + kept(b) for a, b in zip(KY[2], KY[3]))


def layout(count):
    if count == 3:
        rest = NG // 2 - WIDE[1]
        tail = 3 * SHARED - 2 * LANES
        assert 0 <= tail <= rest
        pieces = [(0, f, 0, WIDE[0], HALF * f) for f in range(3)]
        pieces += [(1, 2, 0, WIDE[1], 3 * HALF), (2, 2, SHARED - tail, tail, 3 * HALF + WIDE[1])]
        pieces += [(1, f, 0, WIDE[1], 4 * HALF + HALF * f) for f in range(2)]
        start = 6 * HALF
        pieces += [(2, f, 0, SHARED - (tail if f == 2 else 0), start + SHARED * f) for f in range(3)]
        size = start + 2 * LANES
    else:
        pieces = [(0, f, 0, WIDE[0], HALF * f) for f in range(4)]
        pieces += [(1, f, 0, WIDE[1], HALF * (4 + f)) for f in range(4)]
        pieces += [(2, f, 0, SHARED, 8 * HALF + 96 * f) for f in range(4)]
        size = 7 * LANES
    cut = []
    for kind, field, first, lanes, place in pieces:
        while lanes:
            step = min(lanes, LANES - place % LANES)
            cut.append((kind, field, first, step, place))
            first, lanes, place = first + step, lanes - step, place + step
    return cut, size


@functools.lru_cache(None)
def lane_rows():
    out = np.full((8, 2 * LANES), NO_LINE, np.int32)
    for rows in range(2):
        out[rows, HALF * rows : HALF * rows + WIDE[rows]] = np.arange(WIDE[rows])
    out[2, LANES : LANES + SHARED] = np.arange(SHARED)
    out[3, LANES : LANES + SHARED] = np.arange(SHARED)[::-1]
    return out


def turn(a, b):
    angle = (np.asarray(a)[:, None] * np.asarray(b)[None, :]) % NG * (2.0 * np.pi / NG)
    return np.cos(angle), np.sin(angle)


def pair(table):
    high = table.astype(np.float32).astype(ml_dtypes.bfloat16)
    low = (table - high.astype(np.float64)).astype(np.float32).astype(ml_dtypes.bfloat16)
    return np.stack([high, low])


POINTS = np.arange(NG)


@functools.lru_cache(None)
def y_table():
    cosine, sine = turn(np.concatenate(KY), POINTS)
    return np.stack([cosine, -sine], 1).reshape(2 * NG, NG)


def doubled(block):
    return np.kron(np.eye(2), block)


@functools.lru_cache(None)
def z_ahead():
    out = []
    for kz in (np.arange(HALF), np.arange(HALF)[::-1]):
        cosine, sine = turn(POINTS, kz)
        out.append(np.concatenate([doubled(cosine), doubled(sine)], 1))
    return np.concatenate(out, 0)


@functools.lru_cache(None)
def z_back():
    out = []
    for kz in (np.arange(HALF), np.arange(HALF)[::-1]):
        cosine, sine = turn(kz, POINTS)
        weight = np.where(kz == 0, 1.0, 2.0)[:, None]
        cosine, sine = weight * cosine, weight * sine
        sine[kz == 0] = -(1.0 - 2.0 * (POINTS % 2))
        out.append(np.concatenate([doubled(cosine), doubled(sine)], 0))
    return np.concatenate(out, 0)


@functools.lru_cache(None)
def x_tables():
    cosine, sine = turn(POINTS, POINTS)
    ahead = np.zeros((2, NG, N_FFT, 2, SLAB))
    split_planes = lambda table: table.reshape(NG, N_FFT, SLAB)
    ahead[0, :, :, 0] = split_planes(cosine)
    ahead[0, :, :, 1] = split_planes(sine)
    ahead[1, :, :, 0] = split_planes(-sine)
    ahead[1, :, :, 1] = split_planes(cosine)
    ahead = ahead.reshape(2 * NG, 2 * NG)
    return np.concatenate([ahead, ahead.T], 0)


@functools.lru_cache(None)
def mask_rounds():
    edges = {source: [] for source in range(N_FFT)}
    for device in range(N_FFT):
        for rows in range(4):
            index = KY[rows][device] % NG
            edges[index // SLAB].append((device, index % SLAB, rows))
    rounds = []
    for _ in range(SLAB):
        taken = {}

        def place(source, seen):
            for edge in edges[source]:
                if edge[0] in seen:
                    continue
                seen.add(edge[0])
                if edge[0] not in taken or place(taken[edge[0]][0], seen):
                    taken[edge[0]] = (source, edge)
                    return True
            return False

        for source in range(N_FFT):
            assert place(source, set())
        pairs, local, slot = [], [0] * N_FFT, [0] * N_FFT
        for device, (source, edge) in taken.items():
            edges[source].remove(edge)
            pairs.append((source, device))
            local[source] = edge[1]
            slot[device] = edge[2]
        rounds.append((tuple(sorted(pairs)), tuple(local), tuple(slot)))
    return tuple(rounds)


@functools.lru_cache(None)
def device_table():
    out = np.zeros((N_FFT, 16), np.int32)
    for turn_, (_, local, slot) in enumerate(mask_rounds()):
        for device in range(N_FFT):
            ky = KY[slot[device]][device]
            out[device, turn_] = local[device]
            out[device, 4 + turn_] = kept(ky)
            out[device, 8 + turn_] = ky
            out[device, 12 + turn_] = slot[device]
    return out.reshape(-1)


ZERO_ROUND = [slot[0] for _, _, slot in mask_rounds()].index(0)


@functools.lru_cache(None)
def shared_width():
    width = np.repeat(np.asarray([kept(k) for k in KY[2]], np.int32), BLOCK)
    return np.ascontiguousarray(np.broadcast_to(width[:, None], (2 * NG, LANES)))


def split(value):
    high = value.astype(jnp.bfloat16)
    return high, (value - high.astype(jnp.float32)).astype(jnp.bfloat16)


def dot(left, right):
    return jnp.dot(left, right, preferred_element_type=jnp.float32)


def dot3(left, right):
    return dot(left[0], right[0]) + (dot(left[1], right[0]) + dot(left[0], right[1]))


def both(ref, start=0, size=None):
    size = ref.shape[1] if size is None else size
    return ref[0, start : start + size, :], ref[1, start : start + size, :]


def lane_roll(value, shift):
    shift %= LANES
    return value if shift == 0 else pltpu.roll(value, shift, 1)


def parts_swapped(value):
    blocks = value.reshape(-1, BLOCK, value.shape[1])
    return pltpu.roll(blocks, SLAB, 1).reshape(value.shape)


def beside(parts):
    return parts[0] if len(parts) == 1 else jnp.concatenate(parts, axis=1)


def iota(shape, dim):
    return lax.broadcasted_iota(jnp.int32, shape, dim)


def ahead_body(count, products_of, n_in, *refs):
    inputs = refs[:n_in]
    y_ref, z_ref, width_ref, out_ref, *grids = refs[n_in:]
    pieces, size = layout(count)
    fields = products_of(inputs)
    is_imag = iota((2 * NG, LANES), 0) % BLOCK >= SLAB
    sides = {}
    table = both(y_ref)
    for first in range(0, count, 2):
        two = range(first, min(first + 2, count))
        for x in range(SLAB):
            plane = slice(NG * x, NG * x + NG)
            cells = [fields[field](plane) for field in two]
            lines = dot3(table, split(beside(cells)))
            for spot, field in enumerate(two):
                piece = lines[:, NG * spot : NG * (spot + 1)]
                grids[field][pl.ds(x, 2 * NG, stride=SLAB), :] = piece
        for rows in range(4):
            block = slice(2 * NG * rows, 2 * NG * (rows + 1))
            lines = split(beside([grids[field][block, :] for field in two]))
            lines = dot3(lines, both(z_ref, 2 * NG if rows == 3 else 0, NG * len(two)))
            turned = parts_swapped(lines[:, LANES:])
            sides[first // 2, rows] = lines[:, :LANES] + jnp.where(is_imag, -turned, turned)
    lane = iota((2 * NG, LANES), 1)
    shared = {}
    for field in range(count):
        shift = HALF * (field % 2)
        wide = lane_roll(sides[field // 2, 2], -shift)
        narrow = lane_roll(sides[field // 2, 3], SHARED - HALF - shift)
        shared[field] = jnp.where(lane < width_ref[...], wide, narrow)
    tiles = [None] * (size // LANES)
    for kind, field, first, lanes, place in pieces:
        if kind == 2:
            value, shift = shared[field], 0
        else:
            value, shift = sides[field // 2, kind], HALF * (field % 2)
        start = place % LANES
        value = lane_roll(value, start - first - shift)
        old = tiles[place // LANES]
        if old is None:
            old = jnp.zeros_like(value)
        tiles[place // LANES] = jnp.where((lane >= start) & (lane < start + lanes), value, old)
    for tile, value in enumerate(tiles):
        out_ref[:, LANES * tile : LANES * (tile + 1)] = value
    row, column = iota((BLOCK, LANES), 0), iota((BLOCK, LANES), 1)
    sign = (1 - 2 * (iota((1, NG), 1) % 2)).astype(jnp.float32)
    for kind, field, _, _, place in pieces:
        if kind:
            continue
        extra = jnp.zeros((BLOCK, LANES), jnp.float32)
        for x in range(SLAB):
            cells = fields[field](slice(NG * x, NG * x + NG))
            cells = jnp.sum(cells, axis=0, keepdims=True) * sign
            value = jnp.sum(cells, axis=1, keepdims=True)
            extra = jnp.where((row == SLAB + x) & (column == place % LANES), value, extra)
        tile = place // LANES * LANES
        out_ref[0:BLOCK, tile : tile + LANES] += extra


def middle_body(me_ref, device_ref, own_ref, cross_ref, lane_ref, table_ref, *rest):
    *mask_refs, out_ref = rest
    base = me_ref[0] * 16
    spot = (iota((HALF, LANES), 0) == 0) & (iota((HALF, LANES), 1) == HALF - 1)
    masks = []
    for ref in mask_refs:
        cells = ref[...].astype(jnp.float32)
        high = jnp.where(spot, 0.0, pltpu.roll(cells, HALF, 1))
        masks.append(jnp.concatenate([cells, high], axis=0).astype(jnp.bfloat16))
    zero_mask = mask_refs[ZERO_ROUND][0:1, LANES - 1 : LANES].astype(jnp.float32)
    special = zero_mask / ((1.0 + HALF * HALF / (NG * NG / 16.0)) * float(NG**3))
    kx = iota((NG, LANES), 0)
    signed = jnp.where(kx < HALF, kx, kx - NG)
    plain = []
    for lanes in (slice(0, LANES), slice(LANES, 2 * LANES)):
        cells = jnp.zeros((NG, LANES), jnp.float32)
        squared = jnp.zeros((1, LANES), jnp.int32)
        for turn_ in range(4):
            slot = device_ref[base + 12 + turn_]
            kz = lane_ref[0:1, lanes]
            for which in range(1, 4):
                kz = jnp.where(slot == which, lane_ref[which : which + 1, lanes], kz)
            ky = device_ref[base + 8 + turn_]
            chosen = kz < device_ref[base + 4 + turn_]
            spread = jnp.where((kx == kz) & chosen, 1.0, 0.0).astype(jnp.bfloat16)
            cells += dot(masks[turn_], spread)
            squared += jnp.where(chosen, kz * kz + ky * ky, 0)
        squared = (signed * signed + squared).astype(jnp.float32)
        plain.append(cells / ((1.0 + squared / (NG * NG / 16.0)) * float(NG**3)))

    lane = iota((NG, LANES), 1)
    is_imag = iota((2 * NG, LANES), 0) % BLOCK >= SLAB
    forward = both(table_ref, 0, 2 * NG)
    inverse = both(table_ref, 2 * NG, 2 * NG)
    offset = 0
    for count, x_ref in ((3, own_ref), (4, cross_ref)):
        pieces, size = layout(count)
        weights = [jnp.zeros((NG, LANES), jnp.float32) for _ in range(size // LANES)]
        zeros = [[] for _ in weights]
        for kind, _, first, lanes, place in pieces:
            tile, start = place // LANES, place % LANES
            value = lane_roll(plain[kind // 2], start - first - HALF * (kind % 2))
            inside = (lane >= start) & (lane < start + lanes)
            weights[tile] = jnp.where(inside, value, weights[tile])
            if kind == 0:
                zeros[tile].append(start)
        for step in range(0, size, 2 * LANES):
            values, real, imag = [], [], []
            for tile in range(step // LANES, min(step + 2 * LANES, size) // LANES):
                value = x_ref[:, LANES * tile : LANES * (tile + 1)]
                weight = weights[tile]
                real.append(weight)
                if zeros[tile]:
                    at_zero = lane == zeros[tile][0]
                    for start in zeros[tile][1:]:
                        at_zero |= lane == start
                    at_zero &= me_ref[0] == 0
                    mean = jnp.sum(jnp.where(is_imag, value, 0.0), axis=0, keepdims=True)
                    value = jnp.where(is_imag & at_zero[0:1], mean * (1.0 / NG), value)
                    weight = jnp.where((kx == 0) & at_zero, special, weight)
                values.append(value)
                imag.append(weight)
            spectrum = dot3(forward, split(beside(values)))
            weight = jnp.concatenate([beside(real), beside(imag)], axis=0)
            place = offset + step
            width = LANES * len(values)
            out_ref[:, place : place + width] = dot3(inverse, split(spectrum * weight))
        offset += size


def potentials(count, offset, lines_ref, y_ref, z_ref, width_ref, grids):
    pieces, _ = layout(count)
    pieces = [(*piece[:4], piece[4] + offset) for piece in pieces]
    lane = iota((2 * NG, LANES), 1)
    is_imag = iota((2 * NG, LANES), 0) % BLOCK >= SLAB
    sides = {}

    def add(key, value):
        sides[key] = value if key not in sides else sides[key] + value

    shared = {}
    for kind, field, first, lanes, place in pieces:
        tile = place // LANES * LANES
        start = place % LANES
        value = lines_ref[:, tile : tile + LANES]
        value = jnp.where((lane >= start) & (lane < start + lanes), value, 0.0)
        shift = first - start
        if kind == 2:
            value = lane_roll(value, shift)
            shared[field] = value if field not in shared else shared[field] + value
        else:
            add((field // 2, kind), lane_roll(value, shift + HALF * (field % 2)))
    for field, value in shared.items():
        shift = HALF * (field % 2)
        wide = lane < width_ref[...]
        add((field // 2, 2), lane_roll(jnp.where(wide, value, 0.0), shift))
        add((field // 2, 3), lane_roll(jnp.where(wide, 0.0, value), HALF - SHARED + shift))
    for (index, rows), value in sides.items():
        turned = parts_swapped(value)
        value = jnp.concatenate([value, jnp.where(is_imag, turned, -turned)], axis=1)
        table = both(z_ref, 2 * NG if rows == 3 else 0, 2 * NG)
        cells = dot3(split(value), table)
        for field in range(2 * index, min(2 * index + 2, count)):
            block = slice(2 * NG * rows, 2 * NG * (rows + 1))
            grids[field][block, :] = cells[:, NG * (field % 2) : NG * (field % 2 + 1)]
    table = both(y_ref)

    def plane_of(x):
        out = []
        for first in range(0, count, 2):
            two = grids[first : first + 2]
            lines = beside([ref[pl.ds(x, 2 * NG, stride=SLAB), :] for ref in two])
            cells = dot3(table, split(lines))
            out += [cells[:, NG * spot : NG * (spot + 1)] for spot in range(len(two))]
        return out

    return plane_of


def back_body(own_ref, other_ref, lines_ref, y_ref, z_ref, width_ref, out_ref, *grids):
    tables = (lines_ref, y_ref, z_ref, width_ref)
    own_plane = potentials(3, 0, *tables, grids[:3])
    cross_plane = potentials(4, layout(3)[1], *tables, grids[3:])
    for x in range(SLAB):
        plane = slice(NG * x, NG * x + NG)
        own = [own_ref[band, plane, :] for band in range(2)]
        other = [other_ref[band, plane, :] for band in range(2)]
        first, mixed, second = own_plane(x)
        cross = cross_plane(x)
        total = first * own[0] + mixed * own[1] + (cross[0] * other[0] + cross[1] * other[1])
        out_ref[0, plane, :] = -0.5 * total
        total = mixed * own[0] + second * own[1] + (cross[2] * other[0] + cross[3] * other[1])
        out_ref[1, plane, :] = -0.5 * total


def product(left, i, right, j):
    return lambda plane: left[i, plane, :] * right[j, plane, :]


def own_products(refs):
    (own,) = refs
    return [product(own, 0, own, 0), product(own, 0, own, 1), product(own, 1, own, 1)]


def cross_products(refs):
    own, other = refs
    return [product(own, b, other, j) for b in range(2) for j in range(2)]


def mask_body(me_ref, device_ref, mask_ref, *out_refs):
    lane = iota((HALF, LANES), 1)
    for turn_, out_ref in enumerate(out_refs):
        row = device_ref[me_ref[0] * 16 + turn_]
        low = mask_ref[pl.ds(row, HALF, stride=SLAB), :]
        high = mask_ref[pl.ds(row + HALF * SLAB, HALF, stride=SLAB), :]
        packed = jnp.where(lane < HALF, low, pltpu.roll(high, HALF, 1))
        spot = (iota((HALF, LANES), 0) == 0) & (lane == LANES - 1)
        out_ref[...] = jnp.where(spot, low[0:1, HALF : HALF + 1], packed)


def params(limit=VMEM_LIMIT):
    return pltpu.CompilerParams(vmem_limit_bytes=limit)


def cost(flops, moved):
    return pl.CostEstimate(flops=flops, bytes_accessed=moved, transcendentals=0)


def call(body, shape, args, fields, flops, limit, name):
    return pl.pallas_call(
        body,
        out_shape=jax.ShapeDtypeStruct(shape, jnp.float32),
        in_specs=[pl.BlockSpec(memory_space=pltpu.VMEM) for _ in args],
        out_specs=pl.BlockSpec(memory_space=pltpu.VMEM),
        scratch_shapes=[pltpu.VMEM((ROWS_ALL, NG), jnp.float32) for _ in range(fields)],
        compiler_params=params(limit),
        cost_estimate=cost(flops, 4 * 10**6),
        name=name,
    )(*args)


def ahead(count, products_of, grids, flops, limit, name):
    tables = (pair(y_table()), pair(z_ahead()), shared_width())
    args = [*grids, *(jnp.asarray(table) for table in tables)]
    body = functools.partial(ahead_body, count, products_of, len(grids))
    return call(body, (2 * NG, layout(count)[1]), args, count, flops, limit, name)


def back(own, other, values):
    tables = (pair(y_table().T), pair(z_back()), shared_width())
    args = [own, other, values, *(jnp.asarray(table) for table in tables)]
    return call(back_body, (2, SLAB * NG, NG), args, 7, 5 * 10**9, VMEM_LIMIT, "back")


def indexed(body, shapes, args, me, flops, name):
    vmem = lambda: pl.BlockSpec(memory_space=pltpu.VMEM)
    return pl.pallas_call(
        body,
        out_shape=shapes,
        grid_spec=pltpu.PrefetchScalarGridSpec(
            num_scalar_prefetch=2,
            grid=(),
            in_specs=[vmem() for _ in args],
            out_specs=[vmem() for _ in shapes],
        ),
        compiler_params=params(),
        cost_estimate=cost(flops, 2 * 10**6),
        name=name,
    )(me, jnp.asarray(device_table()), *args)


def middle(own, cross, masks, me):
    args = [own, cross, jnp.asarray(lane_rows()), jnp.asarray(pair(x_tables())), *masks]
    shape = jax.ShapeDtypeStruct((2 * NG, own.shape[1] + cross.shape[1]), jnp.float32)
    return indexed(middle_body, [shape], args, me, 4 * 10**9, "middle")[0]


def mask_rows(mask, me):
    shapes = [jax.ShapeDtypeStruct((HALF, NG), jnp.int32)] * SLAB
    return indexed(mask_body, shapes, [mask.reshape(NG * SLAB, NG)], me, 10**6, "mask_rows")


def swap(values):
    size = values.shape[1]
    blocks = values.reshape(N_FFT, BLOCK, size)
    blocks = lax.all_to_all(blocks, "fft", split_axis=0, concat_axis=0, tiled=True)
    return blocks.reshape(2 * NG, size)


def body(orbitals, mask):
    me = lax.axis_index("fft").astype(jnp.int32)[None]
    count = lax.axis_size("band")
    other = lax.ppermute(orbitals, "band", [(i, (i + 1) % count) for i in range(count)])
    own = orbitals.reshape(2, SLAB * NG, NG)
    other = other.reshape(2, SLAB * NG, NG)

    sent_own = ahead(3, own_products, (own,), 2 * 10**10, VMEM_MOST, "ahead_own")
    sent_own, mask = lax.optimization_barrier((sent_own, mask))
    lines_own = swap(sent_own)
    masks = [
        lax.ppermute(rows, "fft", pairs)
        for rows, (pairs, _, _) in zip(mask_rows(mask, me), mask_rounds())
    ]
    sent_cross = ahead(4, cross_products, (own, other), 2 * 10**10, VMEM_LIMIT, "ahead_cross")
    (sent_cross, masks[0], masks[1]) = lax.optimization_barrier((sent_cross, masks[0], masks[1]))
    lines_cross = swap(sent_cross)
    lines = swap(middle(lines_own, lines_cross, masks, me))
    return back(own, other, lines).reshape(orbitals.shape)


def solution(mesh):
    in_specs = (P("band", "fft", None, None), P(None, "fft", None))
    out_specs = P("band", "fft", None, None)
    return jax.shard_map(body, mesh=mesh, in_specs=in_specs, out_specs=out_specs, check_vma=False)
```

```python
import functools
import math

import jax
import jax.numpy as jnp
import ml_dtypes
import numpy as np
from jax import lax
from jax.experimental import pallas as pl
from jax.experimental.pallas import tpu as pltpu
from jax.sharding import PartitionSpec as P

NG = 128
HALF = NG // 2
N_FFT = 32
SLAB = NG // N_FFT
BLOCK = 2 * SLAB
LANES = 128
ROWS_ALL = 4 * 2 * NG
NO_LINE = 999
VMEM_LIMIT = 20 * 1024 * 1024
VMEM_MOST = 56 * 1024 * 1024


def kept(ky):
    return min(HALF, math.isqrt(HALF * HALF - ky * ky) + 1)


N_LO = 4


def row_sets():
    sets = [[], [], [], []]
    for device in range(N_FFT):
        lo, z = divmod(device, N_FFT // N_LO)
        run = SLAB * z + lo
        plain = sorted((run, run - 32), key=abs)
        shared = sorted((run + 32, run - 64), key=abs)
        for rows, ky in zip(sets, plain + shared):
            rows.append(ky)
    return sets


KY = row_sets()
WIDE = [max(kept(k) for k in KY[0]), max(kept(k) for k in KY[1])]
SHARED = max(kept(a) + kept(b) for a, b in zip(KY[2], KY[3]))


def layout(count):
    if count == 3:
        rest = NG // 2 - WIDE[1]
        tail = 3 * SHARED - 2 * LANES
        assert 0 <= tail <= rest
        pieces = [(0, f, 0, WIDE[0], HALF * f) for f in range(3)]
        pieces += [(1, 2, 0, WIDE[1], 3 * HALF), (2, 2, SHARED - tail, tail, 3 * HALF + WIDE[1])]
        pieces += [(1, f, 0, WIDE[1], 4 * HALF + HALF * f) for f in range(2)]
        start = 6 * HALF
        pieces += [(2, f, 0, SHARED - (tail if f == 2 else 0), start + SHARED * f) for f in range(3)]
        size = start + 2 * LANES
    else:
        pieces = [(0, f, 0, WIDE[0], HALF * f) for f in range(4)]
        pieces += [(1, f, 0, WIDE[1], HALF * (4 + f)) for f in range(4)]
        pieces += [(2, f, 0, SHARED, 8 * HALF + 96 * f) for f in range(4)]
        size = 7 * LANES
    cut = []
    for kind, field, first, lanes, place in pieces:
        while lanes:
            step = min(lanes, LANES - place % LANES)
            cut.append((kind, field, first, step, place))
            first, lanes, place = first + step, lanes - step, place + step
    return cut, size


@functools.lru_cache(None)
def lane_rows():
    out = np.full((8, 2 * LANES), NO_LINE, np.int32)
    for rows in range(2):
        out[rows, HALF * rows : HALF * rows + WIDE[rows]] = np.arange(WIDE[rows])
    out[2, LANES : LANES + SHARED] = np.arange(SHARED)
    out[3, LANES : LANES + SHARED] = np.arange(SHARED)[::-1]
    return out


def turn(a, b):
    angle = (np.asarray(a)[:, None] * np.asarray(b)[None, :]) % NG * (2.0 * np.pi / NG)
    return np.cos(angle), np.sin(angle)


def pair(table):
    high = table.astype(np.float32).astype(ml_dtypes.bfloat16)
    low = (table - high.astype(np.float64)).astype(np.float32).astype(ml_dtypes.bfloat16)
    return np.stack([high, low])


POINTS = np.arange(NG)


@functools.lru_cache(None)
def y_table():
    cosine, sine = turn(np.concatenate(KY), POINTS)
    return np.stack([cosine, -sine], 1).reshape(2 * NG, NG)


def doubled(block):
    return np.kron(np.eye(2), block)


@functools.lru_cache(None)
def z_ahead():
    out = []
    for kz in (np.arange(HALF), np.arange(HALF)[::-1]):
        cosine, sine = turn(POINTS, kz)
        out.append(np.concatenate([doubled(cosine), doubled(sine)], 1))
    return np.concatenate(out, 0)


@functools.lru_cache(None)
def z_back():
    out = []
    for kz in (np.arange(HALF), np.arange(HALF)[::-1]):
        cosine, sine = turn(kz, POINTS)
        weight = np.where(kz == 0, 1.0, 2.0)[:, None]
        cosine, sine = weight * cosine, weight * sine
        sine[kz == 0] = -(1.0 - 2.0 * (POINTS % 2))
        out.append(np.concatenate([doubled(cosine), doubled(sine)], 0))
    return np.concatenate(out, 0)


@functools.lru_cache(None)
def x_tables():
    cosine, sine = turn(POINTS, POINTS)
    ahead = np.zeros((2, NG, N_FFT, 2, SLAB))
    split_planes = lambda table: table.reshape(NG, N_FFT, SLAB)
    ahead[0, :, :, 0] = split_planes(cosine)
    ahead[0, :, :, 1] = split_planes(sine)
    ahead[1, :, :, 0] = split_planes(-sine)
    ahead[1, :, :, 1] = split_planes(cosine)
    ahead = ahead.reshape(2 * NG, 2 * NG)
    return np.concatenate([ahead, ahead.T], 0)


@functools.lru_cache(None)
def mask_rounds():
    rounds = []
    step = N_FFT // N_LO
    for turn_ in range(N_LO):
        pairs, local, slot = [], [0] * N_FFT, [0] * N_FFT
        for device in range(N_FFT):
            lo, z = divmod(device, step)
            source = (lo ^ turn_) * step + z
            pairs.append((source, device))
            local[source] = lo
            row = SLAB * source + lo
            ky = row if row < HALF else row - NG
            slot[device] = [KY[rows][device] for rows in range(4)].index(ky)
        rounds.append((tuple(pairs), tuple(local), tuple(slot)))
    return tuple(rounds)


@functools.lru_cache(None)
def device_table():
    out = np.zeros((N_FFT, 16), np.int32)
    for turn_, (_, local, slot) in enumerate(mask_rounds()):
        for device in range(N_FFT):
            ky = KY[slot[device]][device]
            out[device, turn_] = local[device]
            out[device, 4 + turn_] = kept(ky)
            out[device, 8 + turn_] = ky
            out[device, 12 + turn_] = slot[device]
    return out.reshape(-1)


ZERO_ROUND = [slot[0] for _, _, slot in mask_rounds()].index(0)


@functools.lru_cache(None)
def shared_width():
    width = np.repeat(np.asarray([kept(k) for k in KY[2]], np.int32), BLOCK)
    return np.ascontiguousarray(np.broadcast_to(width[:, None], (2 * NG, LANES)))


def split(value):
    high = value.astype(jnp.bfloat16)
    return high, (value - high.astype(jnp.float32)).astype(jnp.bfloat16)


def dot(left, right):
    return jnp.dot(left, right, preferred_element_type=jnp.float32)


def dot3(left, right):
    return dot(left[0], right[0]) + (dot(left[1], right[0]) + dot(left[0], right[1]))


def both(ref, start=0, size=None):
    size = ref.shape[1] if size is None else size
    return ref[0, start : start + size, :], ref[1, start : start + size, :]


def lane_roll(value, shift):
    shift %= LANES
    return value if shift == 0 else pltpu.roll(value, shift, 1)


def parts_swapped(value):
    blocks = value.reshape(-1, BLOCK, value.shape[1])
    return pltpu.roll(blocks, SLAB, 1).reshape(value.shape)


def beside(parts):
    return parts[0] if len(parts) == 1 else jnp.concatenate(parts, axis=1)


def iota(shape, dim):
    return lax.broadcasted_iota(jnp.int32, shape, dim)


def ahead_body(count, products_of, n_in, *refs):
    inputs = refs[:n_in]
    y_ref, z_ref, width_ref, out_ref, *grids = refs[n_in:]
    pieces, size = layout(count)
    before = out_ref.shape[1] - size
    if before:
        *inputs, ready_ref = inputs
        *grids, done = grids
        copy = pltpu.make_async_copy(ready_ref, out_ref.at[:, :before], done)
        copy.start()
    fields = products_of(inputs)
    is_imag = iota((2 * NG, LANES), 0) % BLOCK >= SLAB
    sides = {}
    table = both(y_ref)
    for first in range(0, count, 2):
        two = range(first, min(first + 2, count))
        for x in range(SLAB):
            plane = slice(NG * x, NG * x + NG)
            cells = [fields[field](plane) for field in two]
            lines = dot3(table, split(beside(cells)))
            for spot, field in enumerate(two):
                piece = lines[:, NG * spot : NG * (spot + 1)]
                grids[field][pl.ds(x, 2 * NG, stride=SLAB), :] = piece
        for rows in range(4):
            block = slice(2 * NG * rows, 2 * NG * (rows + 1))
            lines = split(beside([grids[field][block, :] for field in two]))
            lines = dot3(lines, both(z_ref, 2 * NG if rows == 3 else 0, NG * len(two)))
            turned = parts_swapped(lines[:, LANES:])
            sides[first // 2, rows] = lines[:, :LANES] + jnp.where(is_imag, -turned, turned)
    lane = iota((2 * NG, LANES), 1)
    shared = {}
    for field in range(count):
        shift = HALF * (field % 2)
        wide = lane_roll(sides[field // 2, 2], -shift)
        narrow = lane_roll(sides[field // 2, 3], SHARED - HALF - shift)
        shared[field] = jnp.where(lane < width_ref[...], wide, narrow)
    tiles = [None] * (size // LANES)
    for kind, field, first, lanes, place in pieces:
        if kind == 2:
            value, shift = shared[field], 0
        else:
            value, shift = sides[field // 2, kind], HALF * (field % 2)
        start = place % LANES
        value = lane_roll(value, start - first - shift)
        old = tiles[place // LANES]
        if old is None:
            old = jnp.zeros_like(value)
        tiles[place // LANES] = jnp.where((lane >= start) & (lane < start + lanes), value, old)
    for tile, value in enumerate(tiles):
        place = before + LANES * tile
        out_ref[:, place : place + LANES] = value
    row, column = iota((BLOCK, LANES), 0), iota((BLOCK, LANES), 1)
    sign = (1 - 2 * (iota((1, NG), 1) % 2)).astype(jnp.float32)
    for kind, field, _, _, place in pieces:
        if kind:
            continue
        extra = jnp.zeros((BLOCK, LANES), jnp.float32)
        for x in range(SLAB):
            cells = fields[field](slice(NG * x, NG * x + NG))
            cells = jnp.sum(cells, axis=0, keepdims=True) * sign
            value = jnp.sum(cells, axis=1, keepdims=True)
            extra = jnp.where((row == SLAB + x) & (column == place % LANES), value, extra)
        tile = before + place // LANES * LANES
        out_ref[0:BLOCK, tile : tile + LANES] += extra
    if before:
        copy.wait()


def weight_body(me_ref, device_ref, lane_ref, *rest):
    *mask_refs, out_ref = rest
    base = me_ref[0] * 16
    spot = (iota((HALF, LANES), 0) == 0) & (iota((HALF, LANES), 1) == HALF - 1)
    masks = []
    for ref in mask_refs:
        cells = ref[...].astype(jnp.float32)
        high = jnp.where(spot, 0.0, pltpu.roll(cells, HALF, 1))
        masks.append(jnp.concatenate([cells, high], axis=0).astype(jnp.bfloat16))
    zero_mask = mask_refs[ZERO_ROUND][0:1, LANES - 1 : LANES].astype(jnp.float32)
    special = zero_mask / ((1.0 + HALF * HALF / (NG * NG / 16.0)) * float(NG**3))
    kx = iota((NG, LANES), 0)
    lane = iota((NG, LANES), 1)
    signed = jnp.where(kx < HALF, kx, kx - NG)
    for kind in range(2):
        lanes = slice(LANES * kind, LANES * (kind + 1))
        cells = jnp.zeros((NG, LANES), jnp.float32)
        squared = jnp.zeros((1, LANES), jnp.int32)
        for turn_ in range(4):
            slot = device_ref[base + 12 + turn_]
            kz = lane_ref[0:1, lanes]
            for which in range(1, 4):
                kz = jnp.where(slot == which, lane_ref[which : which + 1, lanes], kz)
            ky = device_ref[base + 8 + turn_]
            chosen = kz < device_ref[base + 4 + turn_]
            spread = jnp.where((kx == kz) & chosen, 1.0, 0.0).astype(jnp.bfloat16)
            cells += dot(masks[turn_], spread)
            squared += jnp.where(chosen, kz * kz + ky * ky, 0)
        squared = (signed * signed + squared).astype(jnp.float32)
        weight = cells / ((1.0 + squared / (NG * NG / 16.0)) * float(NG**3))
        out_ref[:NG, lanes] = weight
        if kind == 0:
            weight = jnp.where((kx == 0) & (lane == 0) & (me_ref[0] == 0), special, weight)
        out_ref[NG:, lanes] = weight


def middle_body(me_ref, x_ref, weight_ref, table_ref, out_ref):
    plain = [weight_ref[:, LANES * kind : LANES * (kind + 1)] for kind in range(2)]
    lane = iota((2 * NG, LANES), 1)
    is_imag = iota((2 * NG, LANES), 0) % BLOCK >= SLAB
    forward = both(table_ref, 0, 2 * NG)
    inverse = both(table_ref, 2 * NG, 2 * NG)
    offset = 0
    for count in (3, 4):
        pieces, size = layout(count)
        weights = [jnp.zeros((2 * NG, LANES), jnp.float32) for _ in range(size // LANES)]
        zeros = [[] for _ in weights]
        for kind, _, first, lanes, place in pieces:
            tile, start = place // LANES, place % LANES
            value = lane_roll(plain[kind // 2], start - first - HALF * (kind % 2))
            inside = (lane >= start) & (lane < start + lanes)
            weights[tile] = jnp.where(inside, value, weights[tile])
            if kind == 0:
                zeros[tile].append(start)
        for step in range(0, size, 2 * LANES):
            values = []
            tiles = range(step // LANES, min(step + 2 * LANES, size) // LANES)
            for tile in tiles:
                place = offset + LANES * tile
                value = x_ref[:, place : place + LANES]
                if zeros[tile]:
                    at_zero = lane == zeros[tile][0]
                    for start in zeros[tile][1:]:
                        at_zero |= lane == start
                    at_zero &= me_ref[0] == 0
                    mean = jnp.sum(jnp.where(is_imag, value, 0.0), axis=0, keepdims=True)
                    value = jnp.where(is_imag & at_zero, mean * (1.0 / NG), value)
                values.append(value)
            spectrum = dot3(forward, split(beside(values)))
            weight = beside([weights[tile] for tile in tiles])
            place = offset + step
            width = LANES * len(values)
            out_ref[:, place : place + width] = dot3(inverse, split(spectrum * weight))
        offset += size


def potentials(count, offset, lines_ref, y_ref, z_ref, width_ref, grids):
    pieces, _ = layout(count)
    pieces = [(*piece[:4], piece[4] + offset) for piece in pieces]
    lane = iota((2 * NG, LANES), 1)
    is_imag = iota((2 * NG, LANES), 0) % BLOCK >= SLAB
    sides = {}

    def add(key, value):
        sides[key] = value if key not in sides else sides[key] + value

    shared = {}
    for kind, field, first, lanes, place in pieces:
        tile = place // LANES * LANES
        start = place % LANES
        value = lines_ref[:, tile : tile + LANES]
        value = jnp.where((lane >= start) & (lane < start + lanes), value, 0.0)
        shift = first - start
        if kind == 2:
            value = lane_roll(value, shift)
            shared[field] = value if field not in shared else shared[field] + value
        else:
            add((field // 2, kind), lane_roll(value, shift + HALF * (field % 2)))
    for field, value in shared.items():
        shift = HALF * (field % 2)
        wide = lane < width_ref[...]
        add((field // 2, 2), lane_roll(jnp.where(wide, value, 0.0), shift))
        add((field // 2, 3), lane_roll(jnp.where(wide, 0.0, value), HALF - SHARED + shift))
    for (index, rows), value in sides.items():
        turned = parts_swapped(value)
        value = jnp.concatenate([value, jnp.where(is_imag, turned, -turned)], axis=1)
        table = both(z_ref, 2 * NG if rows == 3 else 0, 2 * NG)
        cells = dot3(split(value), table)
        for field in range(2 * index, min(2 * index + 2, count)):
            block = slice(2 * NG * rows, 2 * NG * (rows + 1))
            grids[field][block, :] = cells[:, NG * (field % 2) : NG * (field % 2 + 1)]
    table = both(y_ref)

    def plane_of(x):
        out = []
        for first in range(0, count, 2):
            two = grids[first : first + 2]
            lines = beside([ref[pl.ds(x, 2 * NG, stride=SLAB), :] for ref in two])
            cells = dot3(table, split(lines))
            out += [cells[:, NG * spot : NG * (spot + 1)] for spot in range(len(two))]
        return out

    return plane_of


def back_body(
    core_ref, own_ref, near_ref, far_ref, lines_ref, y_ref, z_ref, width_ref, out_ref, *grids
):
    partner = partners(core_ref, near_ref, far_ref)
    tables = (lines_ref, y_ref, z_ref, width_ref)
    own_plane = potentials(3, 0, *tables, grids[:3])
    cross_plane = potentials(4, layout(3)[1], *tables, grids[3:])
    for x in range(SLAB):
        plane = slice(NG * x, NG * x + NG)
        own = [own_ref[band, plane, :] for band in range(2)]
        other = [partner(band, plane) for band in range(2)]
        first, mixed, second = own_plane(x)
        cross = cross_plane(x)
        total = first * own[0] + mixed * own[1] + (cross[0] * other[0] + cross[1] * other[1])
        out_ref[0, plane, :] = -0.5 * total
        total = mixed * own[0] + second * own[1] + (cross[2] * other[0] + cross[3] * other[1])
        out_ref[1, plane, :] = -0.5 * total


def own_products(refs):
    (own,) = refs
    mixed = lambda i, j: lambda plane: own[i, plane, :] * own[j, plane, :]
    return [mixed(0, 0), mixed(0, 1), mixed(1, 1)]


def partners(core_ref, near_ref, far_ref):
    return lambda band, plane: jnp.where(
        core_ref[0] == 1, near_ref[band, plane, :], far_ref[band, plane, :]
    )


def cross_products(refs):
    core, own, near, far = refs
    other = partners(core, near, far)
    mixed = lambda b, j: lambda plane: own[b, plane, :] * other(j, plane)
    return [mixed(b, j) for b in range(2) for j in range(2)]


def mask_body(me_ref, device_ref, mask_ref, *out_refs):
    lane = iota((HALF, LANES), 1)
    for turn_, out_ref in enumerate(out_refs):
        row = device_ref[me_ref[0] * 16 + turn_]
        low = mask_ref[pl.ds(row, HALF, stride=SLAB), :]
        high = mask_ref[pl.ds(row + HALF * SLAB, HALF, stride=SLAB), :]
        packed = jnp.where(lane < HALF, low, pltpu.roll(high, HALF, 1))
        spot = (iota((HALF, LANES), 0) == 0) & (lane == LANES - 1)
        out_ref[...] = jnp.where(spot, low[0:1, HALF : HALF + 1], packed)


def params(limit=VMEM_LIMIT):
    return pltpu.CompilerParams(vmem_limit_bytes=limit)


def cost(flops, moved):
    return pl.CostEstimate(flops=flops, bytes_accessed=moved, transcendentals=0)


def call(body, shape, args, fields, flops, limit, name, kinds=None, extra=()):
    spaces = {"v": pltpu.VMEM, "s": pltpu.SMEM, "a": pl.ANY}
    kinds = kinds + "v" * (len(args) - len(kinds)) if kinds else "v" * len(args)
    return pl.pallas_call(
        body,
        out_shape=jax.ShapeDtypeStruct(shape, jnp.float32),
        in_specs=[pl.BlockSpec(memory_space=spaces[kind]) for kind in kinds],
        out_specs=pl.BlockSpec(memory_space=pltpu.VMEM),
        scratch_shapes=[pltpu.VMEM((ROWS_ALL, NG), jnp.float32) for _ in range(fields)] + list(extra),
        compiler_params=params(limit),
        cost_estimate=cost(flops, 4 * 10**6),
        name=name,
    )(*args)


def ahead_tables():
    tables = (pair(y_table()), pair(z_ahead()), shared_width())
    return [jnp.asarray(table) for table in tables]


def ahead_own(own):
    body = functools.partial(ahead_body, 3, own_products, 1)
    shape = (2 * NG, layout(3)[1])
    return call(body, shape, [own, *ahead_tables()], 3, 2 * 10**10, VMEM_MOST, "ahead_own")


def ahead_cross(core, own, near, far, ready):
    body = functools.partial(ahead_body, 4, cross_products, 5)
    shape = (2 * NG, layout(3)[1] + layout(4)[1])
    args = [core, own, near, far, ready, *ahead_tables()]
    semaphore = [pltpu.SemaphoreType.DMA]
    return call(body, shape, args, 4, 5 * 10**9, VMEM_LIMIT, "ahead_cross", "svvva", semaphore)


def back(core, own, near, far, values):
    tables = (pair(y_table().T), pair(z_back()), shared_width())
    args = [core, own, near, far, values, *(jnp.asarray(table) for table in tables)]
    shape = (2, SLAB * NG, NG)
    return call(back_body, shape, args, 7, 5 * 10**9, VMEM_LIMIT, "back", "s")


def indexed(body, shapes, scalars, args, flops, name):
    vmem = lambda: pl.BlockSpec(memory_space=pltpu.VMEM)
    return pl.pallas_call(
        body,
        out_shape=shapes,
        grid_spec=pltpu.PrefetchScalarGridSpec(
            num_scalar_prefetch=len(scalars),
            grid=(),
            in_specs=[vmem() for _ in args],
            out_specs=[vmem() for _ in shapes],
        ),
        compiler_params=params(),
        cost_estimate=cost(flops, 2 * 10**6),
        name=name,
    )(*scalars, *args)


def weights_of(masks, me):
    shape = jax.ShapeDtypeStruct((2 * NG, 2 * LANES), jnp.float32)
    scalars = [me, jnp.asarray(device_table())]
    args = [jnp.asarray(lane_rows()), *masks]
    return indexed(weight_body, [shape], scalars, args, 10**9, "weights")[0]


def middle(values, weights, me):
    args = [values, weights, jnp.asarray(pair(x_tables()))]
    shape = jax.ShapeDtypeStruct(values.shape, jnp.float32)
    return indexed(middle_body, [shape], [me], args, 4 * 10**9, "middle")[0]


def mask_rows(mask, me):
    shapes = [jax.ShapeDtypeStruct((HALF, NG), jnp.int32)] * SLAB
    scalars = [me, jnp.asarray(device_table())]
    return indexed(mask_body, shapes, scalars, [mask.reshape(NG * SLAB, NG)], 10**6, "mask_rows")


def swap(values):
    size = values.shape[1]
    blocks = values.reshape(N_FFT, BLOCK, size)
    blocks = lax.all_to_all(blocks, "fft", split_axis=0, concat_axis=0, tiled=True)
    return blocks.reshape(2 * NG, size)


def body(orbitals, mask):
    me = lax.axis_index("fft").astype(jnp.int32)[None]
    core = (lax.axis_index("band") % 2).astype(jnp.int32)[None]
    count = lax.axis_size("band")
    near = lax.ppermute(orbitals, "band", [(i, i ^ 1) for i in range(count)])
    far = lax.ppermute(near, "band", [(i, (i + 2) % count) for i in range(0, count, 2)])
    shape = (2, SLAB * NG, NG)
    own, near, far = orbitals.reshape(shape), near.reshape(shape), far.reshape(shape)

    sent = ahead_cross(core, own, near, far, ahead_own(own))
    sent, mask = lax.optimization_barrier((sent, mask))
    lines = swap(sent)
    masks = list(mask_rows(mask, me))
    for turn_ in range(1, N_LO):
        masks[turn_] = lax.ppermute(masks[turn_], "fft", mask_rounds()[turn_][0])
    lines = swap(middle(lines, weights_of(masks, me), me))
    return back(core, own, near, far, lines).reshape(orbitals.shape)


def solution(mesh):
    in_specs = (P("band", "fft", None, None), P(None, "fft", None))
    out_specs = P("band", "fft", None, None)
    return jax.shard_map(body, mesh=mesh, in_specs=in_specs, out_specs=out_specs, check_vma=False)
```

```python
import functools
import math

import jax
import jax.numpy as jnp
import ml_dtypes
import numpy as np
from jax import lax
from jax.experimental import pallas as pl
from jax.experimental.pallas import tpu as pltpu
from jax.sharding import PartitionSpec as P

NG = 128
HALF = NG // 2
N_FFT = 32
SLAB = NG // N_FFT
BLOCK = 2 * SLAB
LANES = 128
ROWS_ALL = 4 * 2 * NG
NO_LINE = 999
VMEM_LIMIT = 20 * 1024 * 1024
VMEM_MOST = 56 * 1024 * 1024


def kept(ky):
    return min(HALF, math.isqrt(HALF * HALF - ky * ky) + 1)


N_LO = 4


def row_sets():
    sets = [[], [], [], []]
    for device in range(N_FFT):
        lo, z = divmod(device, N_FFT // N_LO)
        run = SLAB * z + lo
        plain = sorted((run, run - 32), key=abs)
        shared = sorted((run + 32, run - 64), key=abs)
        for rows, ky in zip(sets, plain + shared):
            rows.append(ky)
    return sets


KY = row_sets()
WIDE = [max(kept(k) for k in KY[0]), max(kept(k) for k in KY[1])]
SHARED = max(kept(a) + kept(b) for a, b in zip(KY[2], KY[3]))


def layout(count):
    if count == 3:
        rest = NG // 2 - WIDE[1]
        tail = 3 * SHARED - 2 * LANES
        assert 0 <= tail <= rest
        pieces = [(0, f, 0, WIDE[0], HALF * f) for f in range(3)]
        pieces += [(1, 2, 0, WIDE[1], 3 * HALF), (2, 2, SHARED - tail, tail, 3 * HALF + WIDE[1])]
        pieces += [(1, f, 0, WIDE[1], 4 * HALF + HALF * f) for f in range(2)]
        start = 6 * HALF
        pieces += [(2, f, 0, SHARED - (tail if f == 2 else 0), start + SHARED * f) for f in range(3)]
        size = start + 2 * LANES
    else:
        pieces = [(0, f, 0, WIDE[0], HALF * f) for f in range(4)]
        pieces += [(1, f, 0, WIDE[1], HALF * (4 + f)) for f in range(4)]
        pieces += [(2, f, 0, SHARED, 8 * HALF + 96 * f) for f in range(4)]
        size = 7 * LANES
    cut = []
    for kind, field, first, lanes, place in pieces:
        while lanes:
            step = min(lanes, LANES - place % LANES)
            cut.append((kind, field, first, step, place))
            first, lanes, place = first + step, lanes - step, place + step
    return cut, size


@functools.lru_cache(None)
def lane_rows():
    out = np.full((8, 2 * LANES), NO_LINE, np.int32)
    for rows in range(2):
        out[rows, HALF * rows : HALF * rows + WIDE[rows]] = np.arange(WIDE[rows])
    out[2, LANES : LANES + SHARED] = np.arange(SHARED)
    out[3, LANES : LANES + SHARED] = np.arange(SHARED)[::-1]
    return out


def turn(a, b):
    angle = (np.asarray(a)[:, None] * np.asarray(b)[None, :]) % NG * (2.0 * np.pi / NG)
    return np.cos(angle), np.sin(angle)


def pair(table):
    high = table.astype(np.float32).astype(ml_dtypes.bfloat16)
    low = (table - high.astype(np.float64)).astype(np.float32).astype(ml_dtypes.bfloat16)
    return np.stack([high, low])


POINTS = np.arange(NG)


@functools.lru_cache(None)
def y_table():
    cosine, sine = turn(np.concatenate(KY), POINTS)
    return np.stack([cosine, -sine], 1).reshape(2 * NG, NG)


def doubled(block):
    return np.kron(np.eye(2), block)


@functools.lru_cache(None)
def z_ahead():
    out = []
    for kz in (np.arange(HALF), np.arange(HALF)[::-1]):
        cosine, sine = turn(POINTS, kz)
        out.append(np.concatenate([doubled(cosine), doubled(sine)], 1))
    return np.concatenate(out, 0)


@functools.lru_cache(None)
def z_back():
    out = []
    for kz in (np.arange(HALF), np.arange(HALF)[::-1]):
        cosine, sine = turn(kz, POINTS)
        weight = np.where(kz == 0, 1.0, 2.0)[:, None]
        cosine, sine = weight * cosine, weight * sine
        sine[kz == 0] = -(1.0 - 2.0 * (POINTS % 2))
        out.append(np.concatenate([doubled(cosine), doubled(sine)], 0))
    return np.concatenate(out, 0)


@functools.lru_cache(None)
def x_tables():
    cosine, sine = turn(POINTS, POINTS)
    ahead = np.zeros((2, NG, N_FFT, 2, SLAB))
    split_planes = lambda table: table.reshape(NG, N_FFT, SLAB)
    ahead[0, :, :, 0] = split_planes(cosine)
    ahead[0, :, :, 1] = split_planes(sine)
    ahead[1, :, :, 0] = split_planes(-sine)
    ahead[1, :, :, 1] = split_planes(cosine)
    ahead = ahead.reshape(2 * NG, 2 * NG)
    return np.concatenate([ahead, ahead.T], 0)


@functools.lru_cache(None)
def mask_rounds():
    rounds = []
    step = N_FFT // N_LO
    for turn_ in range(N_LO):
        pairs, local, slot = [], [0] * N_FFT, [0] * N_FFT
        for device in range(N_FFT):
            lo, z = divmod(device, step)
            source = (lo ^ turn_) * step + z
            pairs.append((source, device))
            local[source] = lo
            row = SLAB * source + lo
            ky = row if row < HALF else row - NG
            slot[device] = [KY[rows][device] for rows in range(4)].index(ky)
        rounds.append((tuple(pairs), tuple(local), tuple(slot)))
    return tuple(rounds)


@functools.lru_cache(None)
def device_table():
    out = np.zeros((N_FFT, 16), np.int32)
    for turn_, (_, local, slot) in enumerate(mask_rounds()):
        for device in range(N_FFT):
            ky = KY[slot[device]][device]
            out[device, turn_] = local[device]
            out[device, 4 + turn_] = kept(ky)
            out[device, 8 + turn_] = ky
            out[device, 12 + turn_] = slot[device]
    return out.reshape(-1)


ZERO_ROUND = [slot[0] for _, _, slot in mask_rounds()].index(0)


@functools.lru_cache(None)
def shared_width():
    width = np.repeat(np.asarray([kept(k) for k in KY[2]], np.int32), BLOCK)
    return np.ascontiguousarray(np.broadcast_to(width[:, None], (2 * NG, LANES)))


def split(value):
    high = value.astype(jnp.bfloat16)
    return high, (value - high.astype(jnp.float32)).astype(jnp.bfloat16)


def dot(left, right):
    return jnp.dot(left, right, preferred_element_type=jnp.float32)


def dot3(left, right):
    return dot(left[0], right[0]) + (dot(left[1], right[0]) + dot(left[0], right[1]))


def both(ref, start=0, size=None):
    size = ref.shape[1] if size is None else size
    return ref[0, start : start + size, :], ref[1, start : start + size, :]


def lane_roll(value, shift):
    shift %= LANES
    return value if shift == 0 else pltpu.roll(value, shift, 1)


def parts_swapped(value):
    blocks = value.reshape(-1, BLOCK, value.shape[1])
    return pltpu.roll(blocks, SLAB, 1).reshape(value.shape)


def beside(parts):
    return parts[0] if len(parts) == 1 else jnp.concatenate(parts, axis=1)


def iota(shape, dim):
    return lax.broadcasted_iota(jnp.int32, shape, dim)


def ahead_body(count, before, products_of, n_in, *refs):
    inputs = refs[:n_in]
    y_ref, z_ref, width_ref, sent_ref, *grids, out_ref, done = refs[n_in:]
    pieces, size = layout(count)
    fields = products_of(inputs)
    is_imag = iota((2 * NG, LANES), 0) % BLOCK >= SLAB
    sides = {}
    table = both(y_ref)
    for first in range(0, count, 2):
        two = range(first, min(first + 2, count))
        for x in range(SLAB):
            plane = slice(NG * x, NG * x + NG)
            cells = [fields[field](plane) for field in two]
            lines = dot3(table, split(beside(cells)))
            for spot, field in enumerate(two):
                piece = lines[:, NG * spot : NG * (spot + 1)]
                grids[field][pl.ds(x, 2 * NG, stride=SLAB), :] = piece
        for rows in range(4):
            block = slice(2 * NG * rows, 2 * NG * (rows + 1))
            lines = split(beside([grids[field][block, :] for field in two]))
            lines = dot3(lines, both(z_ref, 2 * NG if rows == 3 else 0, NG * len(two)))
            turned = parts_swapped(lines[:, LANES:])
            sides[first // 2, rows] = lines[:, :LANES] + jnp.where(is_imag, -turned, turned)
    lane = iota((2 * NG, LANES), 1)
    shared = {}
    for field in range(count):
        shift = HALF * (field % 2)
        wide = lane_roll(sides[field // 2, 2], -shift)
        narrow = lane_roll(sides[field // 2, 3], SHARED - HALF - shift)
        shared[field] = jnp.where(lane < width_ref[...], wide, narrow)
    tiles = [None] * (size // LANES)
    for kind, field, first, lanes, place in pieces:
        if kind == 2:
            value, shift = shared[field], 0
        else:
            value, shift = sides[field // 2, kind], HALF * (field % 2)
        start = place % LANES
        value = lane_roll(value, start - first - shift)
        old = tiles[place // LANES]
        if old is None:
            old = jnp.zeros_like(value)
        tiles[place // LANES] = jnp.where((lane >= start) & (lane < start + lanes), value, old)
    row, column = iota((BLOCK, LANES), 0), iota((BLOCK, LANES), 1)
    sign = (1 - 2 * (iota((1, NG), 1) % 2)).astype(jnp.float32)
    extras = {}
    for kind, field, _, _, place in pieces:
        if kind:
            continue
        extra = extras.get(place // LANES, jnp.zeros((BLOCK, LANES), jnp.float32))
        for x in range(SLAB):
            cells = fields[field](slice(NG * x, NG * x + NG))
            cells = jnp.sum(cells, axis=0, keepdims=True) * sign
            value = jnp.sum(cells, axis=1, keepdims=True)
            extra = jnp.where((row == SLAB + x) & (column == place % LANES), value, extra)
        extras[place // LANES] = extra
    copies = []
    for tile, value in enumerate(tiles):
        lanes = slice(LANES * tile, LANES * (tile + 1))
        out_ref[:, lanes] = value
        if tile in extras:
            out_ref[0:BLOCK, lanes] += extras[tile]
        start = before + LANES * tile
        target = sent_ref.at[:, start : start + LANES]
        copies.append(pltpu.make_async_copy(out_ref.at[:, lanes], target, done.at[tile]))
        copies[-1].start()
    for copy in copies:
        copy.wait()


def weight_body(me_ref, device_ref, lane_ref, *rest):
    *mask_refs, out_ref = rest
    base = me_ref[0] * 16
    spot = (iota((HALF, LANES), 0) == 0) & (iota((HALF, LANES), 1) == HALF - 1)
    masks = []
    for ref in mask_refs:
        cells = ref[...].astype(jnp.float32)
        high = jnp.where(spot, 0.0, pltpu.roll(cells, HALF, 1))
        masks.append(jnp.concatenate([cells, high], axis=0).astype(jnp.bfloat16))
    zero_mask = mask_refs[ZERO_ROUND][0:1, LANES - 1 : LANES].astype(jnp.float32)
    special = zero_mask / ((1.0 + HALF * HALF / (NG * NG / 16.0)) * float(NG**3))
    kx = iota((NG, LANES), 0)
    lane = iota((NG, LANES), 1)
    signed = jnp.where(kx < HALF, kx, kx - NG)
    for kind in range(2):
        lanes = slice(LANES * kind, LANES * (kind + 1))
        cells = jnp.zeros((NG, LANES), jnp.float32)
        squared = jnp.zeros((1, LANES), jnp.int32)
        for turn_ in range(4):
            slot = device_ref[base + 12 + turn_]
            kz = lane_ref[0:1, lanes]
            for which in range(1, 4):
                kz = jnp.where(slot == which, lane_ref[which : which + 1, lanes], kz)
            ky = device_ref[base + 8 + turn_]
            chosen = kz < device_ref[base + 4 + turn_]
            spread = jnp.where((kx == kz) & chosen, 1.0, 0.0).astype(jnp.bfloat16)
            cells += dot(masks[turn_], spread)
            squared += jnp.where(chosen, kz * kz + ky * ky, 0)
        squared = (signed * signed + squared).astype(jnp.float32)
        weight = cells / ((1.0 + squared / (NG * NG / 16.0)) * float(NG**3))
        out_ref[:NG, lanes] = weight
        if kind == 0:
            weight = jnp.where((kx == 0) & (lane == 0) & (me_ref[0] == 0), special, weight)
        out_ref[NG:, lanes] = weight


def middle_body(me_ref, x_ref, weight_ref, table_ref, out_ref):
    plain = [weight_ref[:, LANES * kind : LANES * (kind + 1)] for kind in range(2)]
    lane = iota((2 * NG, LANES), 1)
    is_imag = iota((2 * NG, LANES), 0) % BLOCK >= SLAB
    forward = both(table_ref, 0, 2 * NG)
    inverse = both(table_ref, 2 * NG, 2 * NG)
    offset = 0
    for count in (3, 4):
        pieces, size = layout(count)
        weights = [jnp.zeros((2 * NG, LANES), jnp.float32) for _ in range(size // LANES)]
        zeros = [[] for _ in weights]
        for kind, _, first, lanes, place in pieces:
            tile, start = place // LANES, place % LANES
            value = lane_roll(plain[kind // 2], start - first - HALF * (kind % 2))
            inside = (lane >= start) & (lane < start + lanes)
            weights[tile] = jnp.where(inside, value, weights[tile])
            if kind == 0:
                zeros[tile].append(start)
        for step in range(0, size, 2 * LANES):
            values = []
            tiles = range(step // LANES, min(step + 2 * LANES, size) // LANES)
            for tile in tiles:
                place = offset + LANES * tile
                value = x_ref[:, place : place + LANES]
                if zeros[tile]:
                    at_zero = lane == zeros[tile][0]
                    for start in zeros[tile][1:]:
                        at_zero |= lane == start
                    at_zero &= me_ref[0] == 0
                    mean = jnp.sum(jnp.where(is_imag, value, 0.0), axis=0, keepdims=True)
                    value = jnp.where(is_imag & at_zero, mean * (1.0 / NG), value)
                values.append(value)
            spectrum = dot3(forward, split(beside(values)))
            weight = beside([weights[tile] for tile in tiles])
            place = offset + step
            width = LANES * len(values)
            out_ref[:, place : place + width] = dot3(inverse, split(spectrum * weight))
        offset += size


def potentials(count, offset, lines_ref, y_ref, z_ref, width_ref, grids):
    pieces, _ = layout(count)
    pieces = [(*piece[:4], piece[4] + offset) for piece in pieces]
    lane = iota((2 * NG, LANES), 1)
    is_imag = iota((2 * NG, LANES), 0) % BLOCK >= SLAB
    sides = {}

    def add(key, value):
        sides[key] = value if key not in sides else sides[key] + value

    shared = {}
    for kind, field, first, lanes, place in pieces:
        tile = place // LANES * LANES
        start = place % LANES
        value = lines_ref[:, tile : tile + LANES]
        value = jnp.where((lane >= start) & (lane < start + lanes), value, 0.0)
        shift = first - start
        if kind == 2:
            value = lane_roll(value, shift)
            shared[field] = value if field not in shared else shared[field] + value
        else:
            add((field // 2, kind), lane_roll(value, shift + HALF * (field % 2)))
    for field, value in shared.items():
        shift = HALF * (field % 2)
        wide = lane < width_ref[...]
        add((field // 2, 2), lane_roll(jnp.where(wide, value, 0.0), shift))
        add((field // 2, 3), lane_roll(jnp.where(wide, 0.0, value), HALF - SHARED + shift))
    for (index, rows), value in sides.items():
        turned = parts_swapped(value)
        value = jnp.concatenate([value, jnp.where(is_imag, turned, -turned)], axis=1)
        table = both(z_ref, 2 * NG if rows == 3 else 0, 2 * NG)
        cells = dot3(split(value), table)
        for field in range(2 * index, min(2 * index + 2, count)):
            block = slice(2 * NG * rows, 2 * NG * (rows + 1))
            grids[field][block, :] = cells[:, NG * (field % 2) : NG * (field % 2 + 1)]
    table = both(y_ref)

    def plane_of(x):
        out = []
        for first in range(0, count, 2):
            two = grids[first : first + 2]
            lines = beside([ref[pl.ds(x, 2 * NG, stride=SLAB), :] for ref in two])
            cells = dot3(table, split(lines))
            out += [cells[:, NG * spot : NG * (spot + 1)] for spot in range(len(two))]
        return out

    return plane_of


def back_body(
    core_ref, own_ref, near_ref, far_ref, lines_ref, y_ref, z_ref, width_ref, out_ref, *grids
):
    partner = partners(core_ref, near_ref, far_ref)
    tables = (lines_ref, y_ref, z_ref, width_ref)
    own_plane = potentials(3, 0, *tables, grids[:3])
    cross_plane = potentials(4, layout(3)[1], *tables, grids[3:])
    for x in range(SLAB):
        plane = slice(NG * x, NG * x + NG)
        own = [own_ref[band, plane, :] for band in range(2)]
        other = [partner(band, plane) for band in range(2)]
        first, mixed, second = own_plane(x)
        cross = cross_plane(x)
        total = first * own[0] + mixed * own[1] + (cross[0] * other[0] + cross[1] * other[1])
        out_ref[0, plane, :] = -0.5 * total
        total = mixed * own[0] + second * own[1] + (cross[2] * other[0] + cross[3] * other[1])
        out_ref[1, plane, :] = -0.5 * total


def own_products(refs):
    (own,) = refs
    mixed = lambda i, j: lambda plane: own[i, plane, :] * own[j, plane, :]
    return [mixed(0, 0), mixed(0, 1), mixed(1, 1)]


def partners(core_ref, near_ref, far_ref):
    return lambda band, plane: jnp.where(
        core_ref[0] == 1, near_ref[band, plane, :], far_ref[band, plane, :]
    )


def cross_products(refs):
    core, own, near, far, _ = refs
    other = partners(core, near, far)
    mixed = lambda b, j: lambda plane: own[b, plane, :] * other(j, plane)
    return [mixed(b, j) for b in range(2) for j in range(2)]


def mask_body(me_ref, device_ref, mask_ref, *out_refs):
    lane = iota((HALF, LANES), 1)
    for turn_, out_ref in enumerate(out_refs):
        row = device_ref[me_ref[0] * 16 + turn_]
        low = mask_ref[pl.ds(row, HALF, stride=SLAB), :]
        high = mask_ref[pl.ds(row + HALF * SLAB, HALF, stride=SLAB), :]
        packed = jnp.where(lane < HALF, low, pltpu.roll(high, HALF, 1))
        spot = (iota((HALF, LANES), 0) == 0) & (lane == LANES - 1)
        out_ref[...] = jnp.where(spot, low[0:1, HALF : HALF + 1], packed)


def params(limit=VMEM_LIMIT):
    return pltpu.CompilerParams(vmem_limit_bytes=limit)


def cost(flops, moved):
    return pl.CostEstimate(flops=flops, bytes_accessed=moved, transcendentals=0)


def call(body, shape, args, fields, flops, limit, name, kinds="", sent=None):
    spaces = {"v": pltpu.VMEM, "s": pltpu.SMEM, "a": pl.ANY}
    kinds += "v" * (len(args) - len(kinds))
    scratch = [pltpu.VMEM((ROWS_ALL, NG), jnp.float32) for _ in range(fields)]
    if sent:
        scratch += [pltpu.VMEM((2 * NG, sent), jnp.float32)]
        scratch += [pltpu.SemaphoreType.DMA((sent // LANES,))]
    return pl.pallas_call(
        body,
        out_shape=jax.ShapeDtypeStruct(shape, jnp.float32),
        in_specs=[pl.BlockSpec(memory_space=spaces[kind]) for kind in kinds],
        out_specs=pl.BlockSpec(memory_space=pl.ANY if sent else pltpu.VMEM),
        scratch_shapes=scratch,
        input_output_aliases={kinds.index("a"): 0} if "a" in kinds else {},
        compiler_params=params(limit),
        cost_estimate=cost(flops, 4 * 10**6),
        name=name,
    )(*args)


def ahead_tables():
    tables = (pair(y_table()), pair(z_ahead()), shared_width())
    return [jnp.asarray(table) for table in tables]


OWN_LANES, CROSS_LANES = layout(3)[1], layout(4)[1]
SENT_SHAPE = (2 * NG, OWN_LANES + CROSS_LANES)


def ahead_own(own):
    body = functools.partial(ahead_body, 3, 0, own_products, 1)
    args = [own, *ahead_tables()]
    return call(body, SENT_SHAPE, args, 3, 2 * 10**10, VMEM_MOST, "ahead_own", sent=OWN_LANES)


def ahead_cross(core, own, near, far, ready):
    body = functools.partial(ahead_body, 4, OWN_LANES, cross_products, 5)
    args = [core, own, near, far, ready, *ahead_tables()]
    return call(
        body, SENT_SHAPE, args, 4, 5 * 10**9, VMEM_MOST, "ahead_cross", "svvva", CROSS_LANES
    )


def back(core, own, near, far, values):
    tables = (pair(y_table().T), pair(z_back()), shared_width())
    args = [core, own, near, far, values, *(jnp.asarray(table) for table in tables)]
    shape = (2, SLAB * NG, NG)
    return call(back_body, shape, args, 7, 5 * 10**9, VMEM_LIMIT, "back", "s")


def indexed(body, shapes, scalars, args, flops, name):
    vmem = lambda: pl.BlockSpec(memory_space=pltpu.VMEM)
    return pl.pallas_call(
        body,
        out_shape=shapes,
        grid_spec=pltpu.PrefetchScalarGridSpec(
            num_scalar_prefetch=len(scalars),
            grid=(),
            in_specs=[vmem() for _ in args],
            out_specs=[vmem() for _ in shapes],
        ),
        compiler_params=params(),
        cost_estimate=cost(flops, 2 * 10**6),
        name=name,
    )(*scalars, *args)


def weights_of(masks, me):
    shape = jax.ShapeDtypeStruct((2 * NG, 2 * LANES), jnp.float32)
    scalars = [me, jnp.asarray(device_table())]
    args = [jnp.asarray(lane_rows()), *masks]
    return indexed(weight_body, [shape], scalars, args, 10**9, "weights")[0]


def middle(values, weights, me):
    args = [values, weights, jnp.asarray(pair(x_tables()))]
    shape = jax.ShapeDtypeStruct(values.shape, jnp.float32)
    return indexed(middle_body, [shape], [me], args, 4 * 10**9, "middle")[0]


def mask_rows(mask, me):
    shapes = [jax.ShapeDtypeStruct((HALF, NG), jnp.int32)] * SLAB
    scalars = [me, jnp.asarray(device_table())]
    return indexed(mask_body, shapes, scalars, [mask.reshape(NG * SLAB, NG)], 10**6, "mask_rows")


def swap(values):
    size = values.shape[1]
    blocks = values.reshape(N_FFT, BLOCK, size)
    blocks = lax.all_to_all(blocks, "fft", split_axis=0, concat_axis=0, tiled=True)
    return blocks.reshape(2 * NG, size)


def body(orbitals, mask):
    me = lax.axis_index("fft").astype(jnp.int32)[None]
    core = (lax.axis_index("band") % 2).astype(jnp.int32)[None]
    count = lax.axis_size("band")
    near = lax.ppermute(orbitals, "band", [(i, i ^ 1) for i in range(count)])
    far = lax.ppermute(near, "band", [(i, (i + 2) % count) for i in range(0, count, 2)])
    shape = (2, SLAB * NG, NG)
    own, near, far = orbitals.reshape(shape), near.reshape(shape), far.reshape(shape)

    sent = ahead_cross(core, own, near, far, ahead_own(own))
    sent, mask = lax.optimization_barrier((sent, mask))
    lines = swap(sent)
    masks = list(mask_rows(mask, me))
    for turn_ in range(1, N_LO):
        masks[turn_] = lax.ppermute(masks[turn_], "fft", mask_rounds()[turn_][0])
    lines = swap(middle(lines, weights_of(masks, me), me))
    return back(core, own, near, far, lines).reshape(orbitals.shape)


def solution(mesh):
    in_specs = (P("band", "fft", None, None), P(None, "fft", None))
    out_specs = P("band", "fft", None, None)
    return jax.shard_map(body, mesh=mesh, in_specs=in_specs, out_specs=out_specs, check_vma=False)
```

```python
import functools
import math

import jax
import jax.numpy as jnp
import ml_dtypes
import numpy as np
from jax import lax
from jax.experimental import pallas as pl
from jax.experimental.pallas import tpu as pltpu
from jax.sharding import PartitionSpec as P

NG = 128
HALF = NG // 2
N_FFT = 32
SLAB = NG // N_FFT
BLOCK = 2 * SLAB
LANES = 128
ROWS_ALL = 4 * 2 * NG
NO_LINE = 999
VMEM_LIMIT = 20 * 1024 * 1024
VMEM_MOST = 56 * 1024 * 1024


def kept(ky):
    return min(HALF, math.isqrt(HALF * HALF - ky * ky) + 1)


N_LO = 4


def row_sets():
    sets = [[], [], [], []]
    for device in range(N_FFT):
        lo, z = divmod(device, N_FFT // N_LO)
        run = SLAB * z + lo
        plain = sorted((run, run - 32), key=abs)
        shared = sorted((run + 32, run - 64), key=abs)
        for rows, ky in zip(sets, plain + shared):
            rows.append(ky)
    return sets


KY = row_sets()
WIDE = [max(kept(k) for k in KY[0]), max(kept(k) for k in KY[1])]
SHARED = max(kept(a) + kept(b) for a, b in zip(KY[2], KY[3]))


def layout(count):
    if count == 3:
        rest = NG // 2 - WIDE[1]
        tail = 3 * SHARED - 2 * LANES
        assert 0 <= tail <= rest
        pieces = [(0, f, 0, WIDE[0], HALF * f) for f in range(3)]
        pieces += [(1, 2, 0, WIDE[1], 3 * HALF), (2, 2, SHARED - tail, tail, 3 * HALF + WIDE[1])]
        pieces += [(1, f, 0, WIDE[1], 4 * HALF + HALF * f) for f in range(2)]
        start = 6 * HALF
        pieces += [(2, f, 0, SHARED - (tail if f == 2 else 0), start + SHARED * f) for f in range(3)]
        size = start + 2 * LANES
    else:
        pieces = [(0, f, 0, WIDE[0], HALF * f) for f in range(4)]
        pieces += [(1, f, 0, WIDE[1], HALF * (4 + f)) for f in range(4)]
        pieces += [(2, f, 0, SHARED, 8 * HALF + 96 * f) for f in range(4)]
        size = 7 * LANES
    cut = []
    for kind, field, first, lanes, place in pieces:
        while lanes:
            step = min(lanes, LANES - place % LANES)
            cut.append((kind, field, first, step, place))
            first, lanes, place = first + step, lanes - step, place + step
    return cut, size


@functools.lru_cache(None)
def lane_rows():
    out = np.full((8, 2 * LANES), NO_LINE, np.int32)
    for rows in range(2):
        out[rows, HALF * rows : HALF * rows + WIDE[rows]] = np.arange(WIDE[rows])
    out[2, LANES : LANES + SHARED] = np.arange(SHARED)
    out[3, LANES : LANES + SHARED] = np.arange(SHARED)[::-1]
    return out


def turn(a, b):
    angle = (np.asarray(a)[:, None] * np.asarray(b)[None, :]) % NG * (2.0 * np.pi / NG)
    return np.cos(angle), np.sin(angle)


def pair(table):
    high = table.astype(np.float32).astype(ml_dtypes.bfloat16)
    low = (table - high.astype(np.float64)).astype(np.float32).astype(ml_dtypes.bfloat16)
    return np.stack([high, low])


POINTS = np.arange(NG)


@functools.lru_cache(None)
def y_table():
    cosine, sine = turn(np.concatenate(KY), POINTS)
    return np.stack([cosine, -sine], 1).reshape(2 * NG, NG)


def doubled(block):
    return np.kron(np.eye(2), block)


@functools.lru_cache(None)
def z_ahead():
    out = []
    for kz in (np.arange(HALF), np.arange(HALF)[::-1]):
        cosine, sine = turn(POINTS, kz)
        out.append(np.concatenate([doubled(cosine), doubled(sine)], 1))
    return np.concatenate(out, 0)


@functools.lru_cache(None)
def z_back():
    out = []
    for kz in (np.arange(HALF), np.arange(HALF)[::-1]):
        cosine, sine = turn(kz, POINTS)
        weight = np.where(kz == 0, 1.0, 2.0)[:, None]
        cosine, sine = weight * cosine, weight * sine
        sine[kz == 0] = -(1.0 - 2.0 * (POINTS % 2))
        out.append(np.concatenate([doubled(cosine), doubled(sine)], 0))
    return np.concatenate(out, 0)


@functools.lru_cache(None)
def x_tables():
    cosine, sine = turn(POINTS, POINTS)
    ahead = np.zeros((2, NG, N_FFT, 2, SLAB))
    split_planes = lambda table: table.reshape(NG, N_FFT, SLAB)
    ahead[0, :, :, 0] = split_planes(cosine)
    ahead[0, :, :, 1] = split_planes(sine)
    ahead[1, :, :, 0] = split_planes(-sine)
    ahead[1, :, :, 1] = split_planes(cosine)
    ahead = ahead.reshape(2 * NG, 2 * NG)
    return np.concatenate([ahead, ahead.T], 0)


@functools.lru_cache(None)
def mask_rounds():
    rounds = []
    step = N_FFT // N_LO
    for turn_ in range(N_LO):
        pairs, local, slot = [], [0] * N_FFT, [0] * N_FFT
        for device in range(N_FFT):
            lo, z = divmod(device, step)
            source = (lo ^ turn_) * step + z
            pairs.append((source, device))
            local[source] = lo
            row = SLAB * source + lo
            ky = row if row < HALF else row - NG
            slot[device] = [KY[rows][device] for rows in range(4)].index(ky)
        rounds.append((tuple(pairs), tuple(local), tuple(slot)))
    return tuple(rounds)


@functools.lru_cache(None)
def device_table():
    out = np.zeros((N_FFT, 16), np.int32)
    for turn_, (_, local, slot) in enumerate(mask_rounds()):
        for device in range(N_FFT):
            ky = KY[slot[device]][device]
            out[device, turn_] = local[device]
            out[device, 4 + turn_] = kept(ky)
            out[device, 8 + turn_] = ky
            out[device, 12 + turn_] = slot[device]
    return out.reshape(-1)


ZERO_ROUND = [slot[0] for _, _, slot in mask_rounds()].index(0)


@functools.lru_cache(None)
def shared_width():
    width = np.repeat(np.asarray([kept(k) for k in KY[2]], np.int32), BLOCK)
    return np.ascontiguousarray(np.broadcast_to(width[:, None], (2 * NG, LANES)))


def split(value):
    high = value.astype(jnp.bfloat16)
    return high, (value - high.astype(jnp.float32)).astype(jnp.bfloat16)


def dot(left, right):
    return jnp.dot(left, right, preferred_element_type=jnp.float32)


def dot3(left, right):
    return dot(left[0], right[0]) + (dot(left[1], right[0]) + dot(left[0], right[1]))


def both(ref, start=0, size=None):
    size = ref.shape[1] if size is None else size
    return ref[0, start : start + size, :], ref[1, start : start + size, :]


def lane_roll(value, shift):
    shift %= LANES
    return value if shift == 0 else pltpu.roll(value, shift, 1)


def parts_swapped(value):
    blocks = value.reshape(-1, BLOCK, value.shape[1])
    return pltpu.roll(blocks, SLAB, 1).reshape(value.shape)


def beside(parts):
    return parts[0] if len(parts) == 1 else jnp.concatenate(parts, axis=1)


def iota(shape, dim):
    return lax.broadcasted_iota(jnp.int32, shape, dim)


def ahead_body(count, before, products_of, n_in, *refs):
    inputs = refs[:n_in]
    y_ref, z_ref, width_ref, sent_ref, *grids, out_ref, done = refs[n_in:]
    pieces, size = layout(count)
    fields = products_of(inputs)
    is_imag = iota((2 * NG, LANES), 0) % BLOCK >= SLAB
    sides = {}
    table = both(y_ref)
    for first in range(0, count, 2):
        two = range(first, min(first + 2, count))
        for x in range(SLAB):
            plane = slice(NG * x, NG * x + NG)
            cells = [fields[field](plane) for field in two]
            lines = dot3(table, split(beside(cells)))
            for spot, field in enumerate(two):
                piece = lines[:, NG * spot : NG * (spot + 1)]
                grids[field][pl.ds(x, 2 * NG, stride=SLAB), :] = piece
        for rows in range(4):
            block = slice(2 * NG * rows, 2 * NG * (rows + 1))
            lines = split(beside([grids[field][block, :] for field in two]))
            lines = dot3(lines, both(z_ref, 2 * NG if rows == 3 else 0, NG * len(two)))
            turned = parts_swapped(lines[:, LANES:])
            sides[first // 2, rows] = lines[:, :LANES] + jnp.where(is_imag, -turned, turned)
    lane = iota((2 * NG, LANES), 1)
    shared = {}
    for field in range(count):
        shift = HALF * (field % 2)
        wide = lane_roll(sides[field // 2, 2], -shift)
        narrow = lane_roll(sides[field // 2, 3], SHARED - HALF - shift)
        shared[field] = jnp.where(lane < width_ref[...], wide, narrow)
    tiles = [None] * (size // LANES)
    for kind, field, first, lanes, place in pieces:
        if kind == 2:
            value, shift = shared[field], 0
        else:
            value, shift = sides[field // 2, kind], HALF * (field % 2)
        start = place % LANES
        value = lane_roll(value, start - first - shift)
        old = tiles[place // LANES]
        if old is None:
            old = jnp.zeros_like(value)
        tiles[place // LANES] = jnp.where((lane >= start) & (lane < start + lanes), value, old)
    row, column = iota((BLOCK, LANES), 0), iota((BLOCK, LANES), 1)
    sign = (1 - 2 * (iota((1, NG), 1) % 2)).astype(jnp.float32)
    extras = {}
    for kind, field, _, _, place in pieces:
        if kind:
            continue
        extra = extras.get(place // LANES, jnp.zeros((BLOCK, LANES), jnp.float32))
        for x in range(SLAB):
            cells = fields[field](slice(NG * x, NG * x + NG))
            cells = jnp.sum(cells, axis=0, keepdims=True) * sign
            value = jnp.sum(cells, axis=1, keepdims=True)
            extra = jnp.where((row == SLAB + x) & (column == place % LANES), value, extra)
        extras[place // LANES] = extra
    copies = []
    for tile, value in enumerate(tiles):
        lanes = slice(LANES * tile, LANES * (tile + 1))
        out_ref[:, lanes] = value
        if tile in extras:
            out_ref[0:BLOCK, lanes] += extras[tile]
        start = before + LANES * tile
        target = sent_ref.at[:, start : start + LANES]
        copies.append(pltpu.make_async_copy(out_ref.at[:, lanes], target, done.at[tile]))
        copies[-1].start()
    for copy in copies:
        copy.wait()


def weight_body(me_ref, device_ref, lane_ref, *rest):
    *mask_refs, out_ref = rest
    base = me_ref[0] * 16
    spot = (iota((HALF, LANES), 0) == 0) & (iota((HALF, LANES), 1) == HALF - 1)
    masks = []
    for ref in mask_refs:
        cells = ref[...].astype(jnp.float32)
        high = jnp.where(spot, 0.0, pltpu.roll(cells, HALF, 1))
        masks.append(jnp.concatenate([cells, high], axis=0).astype(jnp.bfloat16))
    zero_mask = mask_refs[ZERO_ROUND][0:1, LANES - 1 : LANES].astype(jnp.float32)
    special = zero_mask / ((1.0 + HALF * HALF / (NG * NG / 16.0)) * float(NG**3))
    kx = iota((NG, LANES), 0)
    lane = iota((NG, LANES), 1)
    signed = jnp.where(kx < HALF, kx, kx - NG)
    for kind in range(2):
        lanes = slice(LANES * kind, LANES * (kind + 1))
        cells = jnp.zeros((NG, LANES), jnp.float32)
        squared = jnp.zeros((1, LANES), jnp.int32)
        for turn_ in range(4):
            slot = device_ref[base + 12 + turn_]
            kz = lane_ref[0:1, lanes]
            for which in range(1, 4):
                kz = jnp.where(slot == which, lane_ref[which : which + 1, lanes], kz)
            ky = device_ref[base + 8 + turn_]
            chosen = kz < device_ref[base + 4 + turn_]
            spread = jnp.where((kx == kz) & chosen, 1.0, 0.0).astype(jnp.bfloat16)
            cells += dot(masks[turn_], spread)
            squared += jnp.where(chosen, kz * kz + ky * ky, 0)
        squared = (signed * signed + squared).astype(jnp.float32)
        weight = cells / ((1.0 + squared / (NG * NG / 16.0)) * float(NG**3))
        out_ref[:NG, lanes] = weight
        if kind == 0:
            weight = jnp.where((kx == 0) & (lane == 0) & (me_ref[0] == 0), special, weight)
        out_ref[NG:, lanes] = weight


def middle_body(me_ref, x_ref, weight_ref, table_ref, out_ref):
    plain = [weight_ref[:, LANES * kind : LANES * (kind + 1)] for kind in range(2)]
    lane = iota((2 * NG, LANES), 1)
    is_imag = iota((2 * NG, LANES), 0) % BLOCK >= SLAB
    forward = both(table_ref, 0, 2 * NG)
    inverse = both(table_ref, 2 * NG, 2 * NG)
    offset = 0
    for count in (3, 4):
        pieces, size = layout(count)
        weights = [jnp.zeros((2 * NG, LANES), jnp.float32) for _ in range(size // LANES)]
        zeros = [[] for _ in weights]
        for kind, _, first, lanes, place in pieces:
            tile, start = place // LANES, place % LANES
            value = lane_roll(plain[kind // 2], start - first - HALF * (kind % 2))
            inside = (lane >= start) & (lane < start + lanes)
            weights[tile] = jnp.where(inside, value, weights[tile])
            if kind == 0:
                zeros[tile].append(start)
        for step in range(0, size, 2 * LANES):
            values = []
            tiles = range(step // LANES, min(step + 2 * LANES, size) // LANES)
            for tile in tiles:
                place = offset + LANES * tile
                value = x_ref[:, place : place + LANES]
                if zeros[tile]:
                    at_zero = lane == zeros[tile][0]
                    for start in zeros[tile][1:]:
                        at_zero |= lane == start
                    at_zero &= me_ref[0] == 0
                    mean = jnp.sum(jnp.where(is_imag, value, 0.0), axis=0, keepdims=True)
                    value = jnp.where(is_imag & at_zero, mean * (1.0 / NG), value)
                values.append(value)
            spectrum = dot3(forward, split(beside(values)))
            weight = beside([weights[tile] for tile in tiles])
            place = offset + step
            width = LANES * len(values)
            out_ref[:, place : place + width] = dot3(inverse, split(spectrum * weight))
        offset += size


def potentials(count, offset, lines_ref, y_ref, z_ref, width_ref, grids):
    pieces, _ = layout(count)
    pieces = [(*piece[:4], piece[4] + offset) for piece in pieces]
    lane = iota((2 * NG, LANES), 1)
    is_imag = iota((2 * NG, LANES), 0) % BLOCK >= SLAB
    sides = {}

    def add(key, value):
        sides[key] = value if key not in sides else sides[key] + value

    shared = {}
    for kind, field, first, lanes, place in pieces:
        tile = place // LANES * LANES
        start = place % LANES
        value = lines_ref[:, tile : tile + LANES]
        value = jnp.where((lane >= start) & (lane < start + lanes), value, 0.0)
        shift = first - start
        if kind == 2:
            value = lane_roll(value, shift)
            shared[field] = value if field not in shared else shared[field] + value
        else:
            add((field // 2, kind), lane_roll(value, shift + HALF * (field % 2)))
    for field, value in shared.items():
        shift = HALF * (field % 2)
        wide = lane < width_ref[...]
        add((field // 2, 2), lane_roll(jnp.where(wide, value, 0.0), shift))
        add((field // 2, 3), lane_roll(jnp.where(wide, 0.0, value), HALF - SHARED + shift))
    for (index, rows), value in sides.items():
        turned = parts_swapped(value)
        value = jnp.concatenate([value, jnp.where(is_imag, turned, -turned)], axis=1)
        table = both(z_ref, 2 * NG if rows == 3 else 0, 2 * NG)
        cells = dot3(split(value), table)
        for field in range(2 * index, min(2 * index + 2, count)):
            block = slice(2 * NG * rows, 2 * NG * (rows + 1))
            grids[field][block, :] = cells[:, NG * (field % 2) : NG * (field % 2 + 1)]
    table = both(y_ref)

    def plane_of(x):
        out = []
        for first in range(0, count, 2):
            two = grids[first : first + 2]
            lines = beside([ref[pl.ds(x, 2 * NG, stride=SLAB), :] for ref in two])
            cells = dot3(table, split(lines))
            out += [cells[:, NG * spot : NG * (spot + 1)] for spot in range(len(two))]
        return out

    return plane_of


def back_body(
    core_ref, own_ref, near_ref, far_ref, lines_ref, y_ref, z_ref, width_ref, sent_ref, *grids
):
    *grids, out_ref, done = grids
    copies = []
    partner = partners(core_ref, near_ref, far_ref)
    tables = (lines_ref, y_ref, z_ref, width_ref)
    own_plane = potentials(3, 0, *tables, grids[:3])
    cross_plane = potentials(4, layout(3)[1], *tables, grids[3:])
    for x in range(SLAB):
        plane = slice(NG * x, NG * x + NG)
        own = [own_ref[band, plane, :] for band in range(2)]
        other = [partner(band, plane) for band in range(2)]
        first, mixed, second = own_plane(x)
        cross = cross_plane(x)
        total = first * own[0] + mixed * own[1] + (cross[0] * other[0] + cross[1] * other[1])
        out_ref[0, plane, :] = -0.5 * total
        total = mixed * own[0] + second * own[1] + (cross[2] * other[0] + cross[3] * other[1])
        out_ref[1, plane, :] = -0.5 * total
        target = sent_ref.at[:, plane, :]
        copies.append(pltpu.make_async_copy(out_ref.at[:, plane, :], target, done.at[x]))
        copies[-1].start()
    for copy in copies:
        copy.wait()


def own_products(refs):
    (own,) = refs
    mixed = lambda i, j: lambda plane: own[i, plane, :] * own[j, plane, :]
    return [mixed(0, 0), mixed(0, 1), mixed(1, 1)]


def partners(core_ref, near_ref, far_ref):
    return lambda band, plane: jnp.where(
        core_ref[0] == 1, near_ref[band, plane, :], far_ref[band, plane, :]
    )


def cross_products(refs):
    core, own, near, far, _ = refs
    other = partners(core, near, far)
    mixed = lambda b, j: lambda plane: own[b, plane, :] * other(j, plane)
    return [mixed(b, j) for b in range(2) for j in range(2)]


def mask_body(me_ref, device_ref, mask_ref, *out_refs):
    lane = iota((HALF, LANES), 1)
    for turn_, out_ref in enumerate(out_refs):
        row = device_ref[me_ref[0] * 16 + turn_]
        low = mask_ref[pl.ds(row, HALF, stride=SLAB), :]
        high = mask_ref[pl.ds(row + HALF * SLAB, HALF, stride=SLAB), :]
        packed = jnp.where(lane < HALF, low, pltpu.roll(high, HALF, 1))
        spot = (iota((HALF, LANES), 0) == 0) & (lane == LANES - 1)
        out_ref[...] = jnp.where(spot, low[0:1, HALF : HALF + 1], packed)


def params(limit=VMEM_LIMIT):
    return pltpu.CompilerParams(vmem_limit_bytes=limit)


def cost(flops, moved):
    return pl.CostEstimate(flops=flops, bytes_accessed=moved, transcendentals=0)


def call(body, shape, args, fields, flops, limit, name, kinds="", sent=None):
    spaces = {"v": pltpu.VMEM, "s": pltpu.SMEM, "a": pl.ANY}
    kinds += "v" * (len(args) - len(kinds))
    scratch = [pltpu.VMEM((ROWS_ALL, NG), jnp.float32) for _ in range(fields)]
    if sent:
        held, parts = sent
        scratch += [pltpu.VMEM(held, jnp.float32), pltpu.SemaphoreType.DMA((parts,))]
    return pl.pallas_call(
        body,
        out_shape=jax.ShapeDtypeStruct(shape, jnp.float32),
        in_specs=[pl.BlockSpec(memory_space=spaces[kind]) for kind in kinds],
        out_specs=pl.BlockSpec(memory_space=pl.ANY if sent else pltpu.VMEM),
        scratch_shapes=scratch,
        input_output_aliases={kinds.index("a"): 0} if "a" in kinds else {},
        compiler_params=params(limit),
        cost_estimate=cost(flops, 4 * 10**6),
        name=name,
    )(*args)


def ahead_tables():
    tables = (pair(y_table()), pair(z_ahead()), shared_width())
    return [jnp.asarray(table) for table in tables]


OWN_LANES, CROSS_LANES = layout(3)[1], layout(4)[1]
SENT_SHAPE = (2 * NG, OWN_LANES + CROSS_LANES)


def ahead_own(own):
    body = functools.partial(ahead_body, 3, 0, own_products, 1)
    args = [own, *ahead_tables()]
    return call(body, SENT_SHAPE, args, 3, 2 * 10**10, VMEM_MOST, "ahead_own", sent=((2 * NG, OWN_LANES), OWN_LANES // LANES))


def ahead_cross(core, own, near, far, ready):
    body = functools.partial(ahead_body, 4, OWN_LANES, cross_products, 5)
    args = [core, own, near, far, ready, *ahead_tables()]
    sent = ((2 * NG, CROSS_LANES), CROSS_LANES // LANES)
    return call(body, SENT_SHAPE, args, 4, 5 * 10**9, VMEM_MOST, "ahead_cross", "svvva", sent)


def back(core, own, near, far, values):
    tables = (pair(y_table().T), pair(z_back()), shared_width())
    args = [core, own, near, far, values, *(jnp.asarray(table) for table in tables)]
    shape = (2, SLAB * NG, NG)
    return call(back_body, shape, args, 7, 5 * 10**9, VMEM_LIMIT, "back", "s", (shape, SLAB))


def indexed(body, shapes, scalars, args, flops, name):
    vmem = lambda: pl.BlockSpec(memory_space=pltpu.VMEM)
    return pl.pallas_call(
        body,
        out_shape=shapes,
        grid_spec=pltpu.PrefetchScalarGridSpec(
            num_scalar_prefetch=len(scalars),
            grid=(),
            in_specs=[vmem() for _ in args],
            out_specs=[vmem() for _ in shapes],
        ),
        compiler_params=params(),
        cost_estimate=cost(flops, 2 * 10**6),
        name=name,
    )(*scalars, *args)


def weights_of(masks, me):
    shape = jax.ShapeDtypeStruct((2 * NG, 2 * LANES), jnp.float32)
    scalars = [me, jnp.asarray(device_table())]
    args = [jnp.asarray(lane_rows()), *masks]
    return indexed(weight_body, [shape], scalars, args, 10**9, "weights")[0]


def middle(values, weights, me):
    args = [values, weights, jnp.asarray(pair(x_tables()))]
    shape = jax.ShapeDtypeStruct(values.shape, jnp.float32)
    return indexed(middle_body, [shape], [me], args, 4 * 10**9, "middle")[0]


def mask_rows(mask, me):
    shapes = [jax.ShapeDtypeStruct((HALF, NG), jnp.int32)] * SLAB
    scalars = [me, jnp.asarray(device_table())]
    return indexed(mask_body, shapes, scalars, [mask.reshape(NG * SLAB, NG)], 10**6, "mask_rows")


def swap(values):
    size = values.shape[1]
    blocks = values.reshape(N_FFT, BLOCK, size)
    blocks = lax.all_to_all(blocks, "fft", split_axis=0, concat_axis=0, tiled=True)
    return blocks.reshape(2 * NG, size)


def body(orbitals, mask):
    me = lax.axis_index("fft").astype(jnp.int32)[None]
    core = (lax.axis_index("band") % 2).astype(jnp.int32)[None]
    count = lax.axis_size("band")
    near = lax.ppermute(orbitals, "band", [(i, i ^ 1) for i in range(count)])
    far = lax.ppermute(near, "band", [(i, (i + 2) % count) for i in range(0, count, 2)])
    shape = (2, SLAB * NG, NG)
    own, near, far = orbitals.reshape(shape), near.reshape(shape), far.reshape(shape)

    sent = ahead_cross(core, own, near, far, ahead_own(own))
    sent, mask = lax.optimization_barrier((sent, mask))
    lines = swap(sent)
    masks = list(mask_rows(mask, me))
    for turn_ in range(1, N_LO):
        masks[turn_] = lax.ppermute(masks[turn_], "fft", mask_rounds()[turn_][0])
    lines = swap(middle(lines, weights_of(masks, me), me))
    return back(core, own, near, far, lines).reshape(orbitals.shape)


def solution(mesh):
    in_specs = (P("band", "fft", None, None), P(None, "fft", None))
    out_specs = P("band", "fft", None, None)
    return jax.shard_map(body, mesh=mesh, in_specs=in_specs, out_specs=out_specs, check_vma=False)
```
